32 devices in a mesh: dp: 8 (over z, x), expert: 4 (over y, core).
Axes of the slice: x: 2, y: 2, z: 4, core: 2. Of those that a mesh axis runs over, the one named last changes fastest.
Arguments:
- grad_tokens: bfloat16 [4096, 2048], P(('dp', 'expert')), may hold values from -6 to 6
- routes: int32 [4096, 2], P(('dp', 'expert')), may hold values from 0 to 3, all different within a row; in each aligned block of 128 rows (0 to 127, 128 to 255, ...) at most 96 rows name the same one
- combine: bfloat16 [4096, 2], P(('dp', 'expert')), may hold values from 0.099609375 to 1
- down_weight: bfloat16 [4, 768, 2048], P('expert'), may hold values from -0.21875 to 0.21875
- saved_pre: bfloat16 [4, 8, 4, 96, 1536], P('expert', 'dp'), may hold values from -6 to 6
Outputs:
- pre_grad: bfloat16 [4, 8, 4, 96, 1536], P('expert', 'dp')
- down_grad: float32 [4, 1572864], P('expert', 'dp')
- gate_grad: float32 [4096, 2], P(('dp', 'expert'))
The draws below stay inside these ranges and needn't reach their ends.
Inputs may be any that keep to these rules, and one draw needn't show every extreme that they name: In each device's block of 128 tokens no expert is named by more than 96 routes, a bound that some blocks reach; a token's routes name different experts.
All inputs are finite; a program needn't handle non-finite values.
Results may differ from the reference program's by a relative error of at most 0.0029.
Values may be sent and summed in bfloat16 or wider, within the bound.
No kernel may reach another device: no remote copies, remote signals or barrier semaphores. Data moves between devices by JAX's collectives and lax.ppermute only.
A program may use at most 64 MiB of HBM per device.

```python
import math
import jax
import jax.numpy as jnp
import numpy as np
from jax import lax

D = 2048
FF = 768
TOP = 2
TOK_DEV = 128
EXPERTS = 4
CAP = 96
TOKENS = 4096
N_DP = 8
N_EXPERT = 4


def level_of(stream_key, dims, cuts, low, largest):
    def one(dim, parts):
        steps = jax.random.uniform(jax.random.fold_in(jax.random.fold_in(stream_key, 6), dim), (parts,), jnp.float32, low / len(cuts), largest / len(cuts))
        return jnp.repeat(jnp.exp(steps), dims[dim] // parts).reshape((-1,) + (1,) * (len(dims) - dim - 1))

    factor_of = one(*cuts[0])
    for cut in cuts[1:]:
        factor_of = factor_of * one(*cut)
    return factor_of


def shared_out(key, own, number, rows, amount, top, most, slope):
    order = jax.random.permutation(key, amount)
    crowded, ordinary = portions_of(amount, rows * top, most, slope, True), portions_of(amount, rows * top, most, slope, False)
    places = jnp.arange(amount)

    def named(tallies, offset_by):
        used = int((tallies > 0).sum())
        fixed = max(1, used // 4)
        moved = fixed + (places - fixed + offset_by * (used - fixed)) % max(1, amount - fixed)
        return jnp.zeros((amount,), jnp.int32).at[order[jnp.where(places < fixed, places, moved)]].set(jnp.asarray(tallies, jnp.int32))

    tallies = jnp.where(number % 4 == 0, named(crowded, number // 4), named(ordinary, number - number // 4 - 1))
    mixed = jax.random.permutation(jax.random.fold_in(own, 3), amount)
    giver, taker = mixed[0:amount // 2 * 2:2], mixed[1:amount // 2 * 2:2]
    margin = jnp.minimum(tallies[giver] - 1, most - tallies[taker]) // 2
    margin = jnp.where((giver == order[0]) | (taker == order[0]) | (tallies[taker] == 0), 0, jnp.maximum(margin, 0))
    moved = jax.random.randint(jax.random.fold_in(own, 4), (amount // 2,), 0, 1 << 20) % (margin + 1)
    tallies = tallies.at[giver].add(-moved).at[taker].add(moved)
    items = jnp.searchsorted(jnp.cumsum(tallies), jnp.arange(rows * top), side="right").astype(jnp.int32)
    table = items.reshape(top, rows).T
    table = table[jax.random.permutation(jax.random.fold_in(own, 1), rows)]
    offset_by = jax.random.randint(jax.random.fold_in(own, 2), (rows, 1), 0, top)
    return jnp.take_along_axis(table, (jnp.arange(top)[None, :] + offset_by) % top, axis=1)


def portions_of(amount, total, limit, lean, full):
    weights = [(1 << 20) // math.isqrt(standing ** lean) + 1 for standing in range(1, amount + 1)]
    largest = limit if full else min(limit, max(-(-total // amount), total * weights[0] // sum(weights)))
    least = 1 if total - largest >= amount - 1 else 0
    given, rest = [largest] + [least] * (amount - 1), total - largest - least * (amount - 1)
    while rest > 0:
        candidates = [i for i in range(1, amount) if given[i] < largest] or [i for i in range(1, amount) if given[i] < limit]
        whole, remaining = sum([weights[i] for i in candidates]), rest
        for i in candidates:
            extra = min(limit - given[i], max(1, remaining * weights[i] // whole), rest)
            given[i] = given[i] + extra
            rest = rest - extra
    return np.array(given)


def centred(own_key, extent, deviation, most, pieces=(), held_as=jnp.bfloat16):
    drawn = deviation * jax.random.normal(own_key, extent, jnp.float32)
    if pieces:
        drawn = drawn * level_of(own_key, extent, pieces, -0.22, 0.18)
    return jnp.clip(drawn, -most, most).astype(held_as)


def setup_inputs(seed: int = 0) -> dict:
    key_list = jax.random.split(jax.random.key(seed), 6)
    grad_tokens = centred(key_list[0], (TOKENS, D), 1.0, 6.0, ((0, 32),))
    routes_keys = jax.random.split(jax.random.fold_in(key_list[1], 1), TOKENS // TOK_DEV)
    routes_turns = jax.random.permutation(jax.random.fold_in(key_list[1], 3), TOKENS // TOK_DEV)
    routes = jax.vmap(lambda own, number: shared_out(jax.random.fold_in(key_list[1], 2), own, number, TOK_DEV, EXPERTS, TOP, CAP, 2))(routes_keys, routes_turns).reshape((TOKENS, TOP))
    combine = jnp.clip(0.099609375 + 0.9003906 * jax.random.uniform(key_list[2], (TOKENS, TOP), jnp.float32) ** level_of(key_list[2], (TOKENS, TOP), ((0, 32),), -0.2, 0.2), 0.099609375, 1.0).astype(jnp.bfloat16)
    down_weight = centred(key_list[3], (EXPERTS, FF, D), FF ** -0.5, 0.21875, ((0, 4),))
    saved_pre = centred(key_list[4], (EXPERTS, N_DP, N_EXPERT, CAP, 2 * FF), 1.0, 6.0, ((0, 4), (1, 8)))
    return {"grad_tokens": grad_tokens, "routes": routes, "combine": combine, "down_weight": down_weight, "saved_pre": saved_pre}


def reference(grad_tokens, routes, combine, down_weight, saved_pre):
    blocks = N_DP * N_EXPERT
    route_total = TOK_DEV * TOP
    route_rows = routes.reshape(blocks, route_total)
    expert_ids = jnp.arange(EXPERTS, dtype=jnp.int32)
    onehot = (route_rows[:, :, None] == expert_ids[None, None, :]).astype(jnp.int32)
    before = jnp.cumsum(onehot, axis=1) - onehot
    position = jnp.sum(before * onehot, axis=2).astype(jnp.int32)
    slot_id = (route_rows * CAP + position).astype(jnp.int32)
    grad_blocks = grad_tokens.reshape(blocks, TOK_DEV, D)
    weight_blocks = combine.reshape(blocks, route_total).astype(jnp.float32)
    route_order = jnp.arange(route_total, dtype=jnp.int32)

    def one_expert(expert_id):
        target = expert_id * CAP + jnp.arange(CAP, dtype=jnp.int32)
        chosen = target[None, :, None] == slot_id[:, None, :]
        filled = jnp.any(chosen, axis=2)
        route_index = jnp.sum(jnp.where(chosen, route_order[None, None, :], 0), axis=2).astype(jnp.int32)
        token_index = (route_index // TOP).astype(jnp.int32)
        slot_rows = jnp.take_along_axis(grad_blocks, token_index[:, :, None], axis=1)
        slot_rows = jnp.where(filled[:, :, None], slot_rows, jnp.zeros_like(slot_rows))
        slot_weight = jnp.sum(jnp.where(chosen, weight_blocks[:, None, :], 0.0), axis=2)
        flat_rows = slot_rows.reshape(blocks * CAP, D)
        flat_weight = slot_weight.reshape(blocks * CAP)
        raw_grad = jnp.dot(flat_rows, down_weight[expert_id].T, preferred_element_type=jnp.float32)
        pre_acts = saved_pre[expert_id].reshape(blocks * CAP, 2 * FF).astype(jnp.float32)
        gate_pre = pre_acts[:, :FF]
        up_pre = pre_acts[:, FF:]
        logistic = jax.nn.sigmoid(gate_pre)
        activated = gate_pre * logistic
        hidden_act = activated * up_pre
        slot_gate = jnp.sum(hidden_act * raw_grad, axis=1)
        hidden_delta = flat_weight[:, None] * raw_grad
        gate_delta = hidden_delta * up_pre * logistic * (1.0 + gate_pre * (1.0 - logistic))
        up_delta = hidden_delta * activated
        pre_grad = jnp.concatenate([gate_delta, up_delta], axis=1).astype(jnp.bfloat16)
        scaled = (flat_weight[:, None] * hidden_act).astype(jnp.bfloat16)
        weight_term = jnp.dot(scaled.T, flat_rows, preferred_element_type=jnp.float32) / N_DP
        return (pre_grad.reshape(N_DP, N_EXPERT, CAP, 2 * FF), weight_term.reshape(FF * D), slot_gate.reshape(blocks, CAP))

    pre_grad, down_grad, gate_all = lax.map(one_expert, expert_ids)
    gate_table = jnp.transpose(gate_all, (1, 0, 2)).reshape(blocks, EXPERTS * CAP)
    gate_grad = jnp.take_along_axis(gate_table, slot_id, axis=1).reshape(TOKENS, TOP)
    return pre_grad, down_grad, gate_grad
```

```python
import functools

import jax
import jax.numpy as jnp
from jax import lax
from jax.experimental import pallas as pl
from jax.experimental.pallas import tpu as pltpu
from jax.sharding import PartitionSpec as P

F32 = jnp.float32
BF16 = jnp.bfloat16
AXES = ("dp", "expert")
VMEM_LIMIT = 56 * 1024 * 1024
CHUNKS = ((3, "x"), (2, "z"), (3, "x"))


def _send(value, dp_mask, expert_mask):
    dps, experts = lax.axis_size("dp"), lax.axis_size("expert")
    pairs = [
        (d * experts + e, (d ^ dp_mask) * experts + (e ^ expert_mask))
        for d in range(dps)
        for e in range(experts)
    ]
    return lax.ppermute(value, AXES, pairs)


def _choice(info, expert, capacity):
    tokens = info.shape[1]
    first, second = info[0:1, :] == expert, info[1:2, :] == expert
    named = jnp.where(first | second, 1.0, 0.0)
    weight = jnp.where(first, info[2:3, :], 0.0) + jnp.where(second, info[3:4, :], 0.0)
    row = lax.broadcasted_iota(jnp.int32, (tokens, tokens), 0)
    col = lax.broadcasted_iota(jnp.int32, (tokens, tokens), 1)
    earlier = jnp.where(row < col, 1.0, 0.0).astype(BF16)
    position = jnp.dot(
        jnp.broadcast_to(named, (8, tokens)).astype(BF16), earlier, preferred_element_type=F32
    )[0:1, :]
    slot = lax.broadcasted_iota(jnp.int32, (capacity, tokens), 0).astype(F32)
    chosen = jnp.where((slot == position) & (named > 0.0), 1.0, 0.0)
    slot_weight = jnp.sum(chosen * weight, axis=1, keepdims=True)
    return chosen, slot_weight


def _scaled_kernel(n_e, n_d, hidden, where_ref, pre_ref, *refs):
    infos, out_ref, held = refs[:n_e], refs[n_e], refs[n_e + 1]
    d, e = where_ref[0], where_ref[1]
    expert = e.astype(F32)
    capacity = pre_ref.shape[1]
    tokens = infos[0].shape[1]
    rows = hidden // n_d
    for j in range(n_e):
        chosen, slot_weight = _choice(infos[j][...], expert, capacity)
        pre = pre_ref[e ^ j].astype(F32)
        gate, up = pre[:, :hidden], pre[:, hidden:]
        act = gate * jax.nn.sigmoid(gate) * up
        scaled = (slot_weight * act).astype(BF16)
        held[:, j * tokens : (j + 1) * tokens] = lax.dot_general(
            scaled, chosen.astype(BF16), (((0,), (0,)), ((), ())), preferred_element_type=F32
        ).astype(BF16)
    for q in range(n_d):
        start = pl.multiple_of((d ^ q) * rows, 16)
        out_ref[q * rows : (q + 1) * rows, :] = held[pl.ds(start, rows), :]


def _partial_kernel(n_e, keep_blocks, send_blocks, rows, at_ref, *refs):
    tok = jnp.concatenate([r[...] for r in refs[:n_e]], axis=0)
    keep_ref, send_ref = refs[n_e:]
    prod = jnp.dot(at_ref[...], tok, preferred_element_type=F32)
    for p, q in enumerate(keep_blocks):
        keep_ref[p * rows : (p + 1) * rows, :] = prod[q * rows : (q + 1) * rows, :]
    for p, q in enumerate(send_blocks):
        send_ref[p * rows : (p + 1) * rows, :] = prod[q * rows : (q + 1) * rows, :].astype(BF16)


def _slot_kernel(n_e, n_c, hidden, where_ref, pre_ref, w_ref, own_ref, *refs):
    infos, refs = refs[:n_e], refs[n_e:]
    others, refs = refs[: (n_e - 1) * n_c], refs[(n_e - 1) * n_c :]
    pre_grad_ref, back_ref, rows_ref = refs
    e = where_ref[1]
    expert = e.astype(F32)
    capacity = pre_ref.shape[1]
    picks, weights = [], []
    for j in range(n_e):
        chosen, slot_weight = _choice(infos[j][...], expert, capacity)
        picks.append(chosen)
        weights.append(slot_weight)
        parts = [own_ref] if j == 0 else others[(j - 1) * n_c : j * n_c]
        at = 0
        for part in parts:
            width = part.shape[1]
            rows_ref[j * capacity : (j + 1) * capacity, at : at + width] = jnp.dot(
                chosen.astype(BF16), part[...], preferred_element_type=F32
            ).astype(BF16)
            at += width
    tile = 256 if hidden % 256 == 0 else hidden
    gates = [jnp.zeros((capacity, 1), F32) for _ in range(n_e)]
    for h in range(0, hidden, tile):
        raw_all = lax.dot_general(
            rows_ref[...], w_ref[0, h : h + tile, :], (((1,), (1,)), ((), ())), preferred_element_type=F32
        )
        for j in range(n_e):
            raw = raw_all[j * capacity : (j + 1) * capacity, :]
            a = pre_ref[e ^ j, :, h : h + tile].astype(F32)
            u = pre_ref[e ^ j, :, hidden + h : hidden + h + tile].astype(F32)
            s = jax.nn.sigmoid(a)
            silu = a * s
            gates[j] = gates[j] + jnp.sum(silu * u * raw, axis=1, keepdims=True)
            delta = weights[j] * raw
            pre_grad_ref[e ^ j, :, h : h + tile] = (delta * u * s * (1.0 + a * (1.0 - s))).astype(BF16)
            pre_grad_ref[e ^ j, :, hidden + h : hidden + h + tile] = (delta * silu).astype(BF16)
    for j in range(n_e):
        back_ref[e ^ j] = jnp.sum(picks[j] * gates[j], axis=0, keepdims=True)


def _params():
    return pltpu.CompilerParams(vmem_limit_bytes=VMEM_LIMIT)


VM = pl.BlockSpec(memory_space=pltpu.VMEM)
SM = pl.BlockSpec(memory_space=pltpu.SMEM)


def _scaled(n_e, n_d, hidden, where, pre, infos):
    tokens = infos[0].shape[1]
    return pl.pallas_call(
        functools.partial(_scaled_kernel, n_e, n_d, hidden),
        out_shape=jax.ShapeDtypeStruct((hidden, n_e * tokens), BF16),
        in_specs=[SM] + [VM] * (1 + n_e),
        out_specs=VM,
        scratch_shapes=[pltpu.VMEM((hidden, n_e * tokens), BF16)],
        compiler_params=_params(),
        name="scaled_by_token",
    )(where, pre, *infos)


def _partial(at, toks, offset, width, keep_blocks, send_blocks, rows):
    n_e = len(toks)
    tile = 256
    hidden, depth = at.shape
    tokens = toks[0].shape[0]
    first = offset // tile
    specs = [pl.BlockSpec((hidden, depth), lambda i: (0, 0))]
    specs.append(pl.BlockSpec((tokens, tile), lambda i: (0, first + i)))
    specs += [pl.BlockSpec((tokens, tile), lambda i: (0, i))] * (n_e - 1)
    n_keep, n_send = len(keep_blocks) * rows, len(send_blocks) * rows
    return pl.pallas_call(
        functools.partial(_partial_kernel, n_e, keep_blocks, send_blocks, rows),
        grid=(width // tile,),
        out_shape=(
            jax.ShapeDtypeStruct((n_keep, width), F32),
            jax.ShapeDtypeStruct((n_send, width), BF16),
        ),
        in_specs=specs,
        out_specs=(
            pl.BlockSpec((n_keep, tile), lambda i: (0, i)),
            pl.BlockSpec((n_send, tile), lambda i: (0, i)),
        ),
        compiler_params=_params(),
        cost_estimate=pl.CostEstimate(
            flops=2 * hidden * depth * width, bytes_accessed=6 << 20, transcendentals=0
        ),
        name="partial_chunk",
    )(at, *toks)


def _slots(n_e, hidden, where, pre, weight, own, infos, others):
    n_c = len(others) // (n_e - 1)
    capacity = pre.shape[1]
    tokens, width = own.shape
    return pl.pallas_call(
        functools.partial(_slot_kernel, n_e, n_c, hidden),
        out_shape=(
            jax.ShapeDtypeStruct(pre.shape, BF16),
            jax.ShapeDtypeStruct((n_e, 1, tokens), F32),
        ),
        in_specs=[SM] + [VM] * (3 + n_e + len(others)),
        out_specs=(VM, VM),
        scratch_shapes=[pltpu.VMEM((n_e * capacity, width), BF16)],
        compiler_params=_params(),
        cost_estimate=pl.CostEstimate(
            flops=2 * n_e * capacity * width * hidden, bytes_accessed=8 << 20, transcendentals=1 << 19
        ),
        name="slot_gradients",
    )(where, pre, weight, own, *infos, *others)


def _fast(grad_tokens, routes, combine, down_weight, saved_pre):
    n_d, n_e = lax.axis_size("dp"), lax.axis_size("expert")
    tokens, width = grad_tokens.shape
    hidden = down_weight.shape[1]
    rows = hidden // n_d
    where = jnp.stack([lax.axis_index("dp"), lax.axis_index("expert")]).astype(jnp.int32)
    pre = saved_pre.reshape(saved_pre.shape[1:])[0]

    info = jnp.concatenate(
        [routes.T.astype(F32), combine.T.astype(F32), jnp.zeros((4, tokens), F32)], axis=0
    )
    infos = [info] + [_send(info, 0, j) for j in range(1, n_e)]

    top = n_e.bit_length() - 1
    bounds, at = [], 0
    for eighths, order in CHUNKS:
        bounds.append((at, eighths * width // 8, order))
        at += eighths * width // 8
    gathered = []
    for offset, size, _ in bounds:
        held = {0: grad_tokens[:, offset : offset + size]}
        for bit in reversed(range(top)):
            for key in sorted(held):
                held[key | (1 << bit)] = _send(held[key], 0, 1 << bit)
        gathered.append([held[j] for j in range(1, n_e)])

    at_all = _scaled(n_e, n_d, hidden, where, pre, infos)

    rest = tuple(range(2, n_d.bit_length() - 1))
    orders = {"x": ((0,), (1,), rest), "z": ((1,), rest, (0,))}
    state = []
    for (offset, size, order), toks in zip(bounds, gathered):
        stages = orders[order]
        bits = [b for group in stages for b in group]
        blocks = [0]
        for b in bits:
            blocks = [q | (v << b) for q in blocks for v in (0, 1)]
        ways = 1 << len(stages[0])
        kept = len(blocks) // ways
        keep, send = _partial(
            at_all, [grad_tokens] + toks, offset, size, tuple(blocks[:kept]), tuple(blocks[kept:]), rows
        )
        state.append([stages, keep, send])

    finals = [None] * len(state)
    for s in range(3):
        for c, (stages, keep, send) in enumerate(state):
            group = stages[s]
            ways = 1 << len(group)
            kept = keep.shape[0]
            total = keep
            for v in range(1, ways):
                mask = sum(
                    (1 << b) for i, b in enumerate(group) if (v >> (len(group) - 1 - i)) & 1
                )
                got = _send(send[(v - 1) * kept : v * kept], mask, 0)
                total = total + got.astype(F32)
            if s < 2:
                kept //= 1 << len(stages[s + 1])
                state[c][1], state[c][2] = total[:kept], total[kept:].astype(BF16)
            else:
                finals[c] = total * (1.0 / n_d)
    down_grad = jnp.concatenate(finals, axis=1).reshape(1, rows * width)

    others = [g[j] for j in range(n_e - 1) for g in gathered]
    pre_grad, back = _slots(n_e, hidden, where, pre, down_weight, grad_tokens, infos, others)
    returned = lax.all_to_all(back, "expert", split_axis=0, concat_axis=0, tiled=True)
    gate_grad = sum(
        jnp.where(routes.T == k, returned[k], 0.0) for k in range(n_e)
    ).T
    return pre_grad.reshape(saved_pre.shape), down_grad, gate_grad


def _general(grad_tokens, routes, combine, down_weight, saved_pre):
    experts = lax.axis_size("expert")
    tok_rows, route_count = routes.shape
    capacity = saved_pre.shape[3]
    model_width = grad_tokens.shape[1]
    hidden = down_weight.shape[1]
    flat_routes = routes.reshape(-1)
    onehot = (flat_routes[:, None] == jnp.arange(experts, dtype=jnp.int32)[None, :]).astype(jnp.int32)
    before = jnp.cumsum(onehot, axis=0) - onehot
    position = jnp.sum(before * onehot, axis=1)
    slot_id = flat_routes * capacity + position
    slot_grid = jnp.arange(experts * capacity, dtype=jnp.int32)
    chosen = slot_grid[:, None] == slot_id[None, :]
    placing = jnp.any(chosen.reshape(experts * capacity, tok_rows, route_count), axis=2).astype(BF16)
    outgoing = jnp.dot(placing, grad_tokens, preferred_element_type=F32).astype(BF16)
    combine_flat = combine.reshape(-1).astype(F32)
    out_weight = jnp.sum(jnp.where(chosen, combine_flat[None, :], 0.0), axis=1).astype(BF16)
    swap = functools.partial(lax.all_to_all, axis_name="expert", split_axis=0, concat_axis=0, tiled=True)
    slot_rows = swap(outgoing.reshape(experts, capacity, model_width)).reshape(-1, model_width)
    slot_weight = swap(out_weight.reshape(experts, capacity)).reshape(-1).astype(F32)
    raw_grad = lax.dot_general(
        slot_rows, down_weight[0], (((1,), (1,)), ((), ())), preferred_element_type=F32
    )
    pre_acts = saved_pre.reshape(-1, 2 * hidden).astype(F32)
    gate_pre, up_pre = pre_acts[:, :hidden], pre_acts[:, hidden:]
    logistic = jax.nn.sigmoid(gate_pre)
    activated = gate_pre * logistic
    hidden_act = activated * up_pre
    slot_gate = jnp.sum(hidden_act * raw_grad, axis=1)
    hidden_delta = slot_weight[:, None] * raw_grad
    gate_delta = hidden_delta * up_pre * logistic * (1.0 + gate_pre * (1.0 - logistic))
    pre_grad = jnp.concatenate([gate_delta, hidden_delta * activated], axis=1).astype(BF16)
    scaled = (slot_weight[:, None] * hidden_act).astype(BF16)
    whole_term = lax.dot_general(
        scaled, slot_rows, (((0,), (0,)), ((), ())), preferred_element_type=F32
    )
    summed = lax.psum_scatter(whole_term.reshape(-1), "dp", scatter_dimension=0, tiled=True)
    down_grad = (summed / lax.axis_size("dp"))[None]
    returned_flat = swap(slot_gate.reshape(experts, capacity)).reshape(-1)
    gate_flat = jnp.sum(jnp.where(chosen, returned_flat[:, None], 0.0), axis=0)
    return pre_grad.reshape(saved_pre.shape), down_grad, gate_flat.reshape(tok_rows, route_count)


def solution(mesh):
    n_d, n_e = mesh.shape["dp"], mesh.shape["expert"]

    def per_device(grad_tokens, routes, combine, down_weight, saved_pre):
        hidden, width = down_weight.shape[1:]
        whole_tiles = (
            hidden % (16 * n_d) == 0
            and saved_pre.shape[3] % 16 == 0
            and width % 2048 == 0
            and n_d >= 8
            and n_d & (n_d - 1) == 0
            and n_e >= 2
            and n_e & (n_e - 1) == 0
            and routes.shape[1] == 2
        )
        form = _fast if whole_tiles else _general
        return form(grad_tokens, routes, combine, down_weight, saved_pre)

    by_both = P(("dp", "expert"), None)
    by_expert = P("expert", "dp", None, None, None)
    return jax.shard_map(
        per_device,
        mesh=mesh,
        in_specs=(by_both, by_both, by_both, P("expert", None, None), by_expert),
        out_specs=(by_expert, P("expert", "dp"), by_both),
        check_vma=False,
    )
```

```python
import functools

import jax
import jax.numpy as jnp
from jax import lax
from jax.experimental import pallas as pl
from jax.experimental.pallas import tpu as pltpu
from jax.sharding import PartitionSpec as P

F32 = jnp.float32
BF16 = jnp.bfloat16
AXES = ("dp", "expert")
MIB = 1024 * 1024
TILE = 512
INFO_ROWS = 16
ORDERS = ("x", "z", "x", "x")


def _send(value, dp_mask, expert_mask):
    dps, experts = lax.axis_size("dp"), lax.axis_size("expert")
    pairs = [
        (d * experts + e, (d ^ dp_mask) * experts + (e ^ expert_mask))
        for d in range(dps)
        for e in range(experts)
    ]
    return lax.ppermute(value, AXES, pairs)


def _choice(info, expert, capacity):
    tokens = info.shape[1]
    first, second = info[0:1, :] == expert, info[1:2, :] == expert
    named = jnp.where(first | second, 1.0, 0.0)
    weight = jnp.where(first, info[2:3, :], 0.0) + jnp.where(second, info[3:4, :], 0.0)
    row = lax.broadcasted_iota(jnp.int32, (tokens, tokens), 0)
    col = lax.broadcasted_iota(jnp.int32, (tokens, tokens), 1)
    earlier = jnp.where(row < col, 1.0, 0.0).astype(BF16)
    position = jnp.dot(
        jnp.broadcast_to(named, (8, tokens)).astype(BF16), earlier, preferred_element_type=F32
    )[0:1, :]
    slot = lax.broadcasted_iota(jnp.int32, (capacity, tokens), 0).astype(F32)
    chosen = jnp.where((slot == position) & (named > 0.0), 1.0, 0.0)
    slot_weight = jnp.sum(chosen * weight, axis=1, keepdims=True)
    return chosen, slot_weight


def _pack_kernel(tokens, routes_ref, combine_ref, tok_ref, first_ref, rest_ref):
    first_ref[0:tokens, :] = tok_ref[:, :TILE]
    first_ref[tokens:, :] = jnp.zeros((INFO_ROWS, TILE), BF16)
    info = jnp.concatenate(
        [
            routes_ref[...].astype(F32),
            combine_ref[...].astype(F32),
            jnp.zeros((INFO_ROWS - 4, tokens), F32),
        ],
        axis=0,
    )
    first_ref[tokens:, 0:tokens] = info.astype(BF16)
    rest_ref[...] = tok_ref[:, TILE:]


def _activate_kernel(hidden, pre_ref, out_ref):
    for j in range(pre_ref.shape[0]):
        pre = pre_ref[j].astype(F32)
        gate, up = pre[:, :hidden], pre[:, hidden:]
        out_ref[j] = gate * jax.nn.sigmoid(gate) * up


def _info(ref, tokens):
    return ref[tokens : tokens + INFO_ROWS, 0:tokens].astype(F32)


def _split(prod, keep_blocks, send_blocks, rows, keep_ref, send_ref):
    for p, q in enumerate(keep_blocks):
        keep_ref[p * rows : (p + 1) * rows, :] = prod[q * rows : (q + 1) * rows, :]
    for p, q in enumerate(send_blocks):
        send_ref[p * rows : (p + 1) * rows, :] = prod[q * rows : (q + 1) * rows, :].astype(BF16)


def _first_kernel(n_e, n_d, keep_blocks, send_blocks, where_ref, act_ref, *refs):
    firsts, (at_ref, keep_ref, send_ref, held) = refs[:n_e], refs[n_e:]
    d, e = where_ref[0], where_ref[1]
    expert = e.astype(F32)
    capacity, hidden = act_ref.shape[1:]
    tokens = firsts[0].shape[0] - INFO_ROWS
    rows = hidden // n_d
    for j in range(n_e):
        chosen, slot_weight = _choice(_info(firsts[j], tokens), expert, capacity)
        scaled = (slot_weight * act_ref[e ^ j]).astype(BF16)
        held[:, j * tokens : (j + 1) * tokens] = lax.dot_general(
            scaled, chosen.astype(BF16), (((0,), (0,)), ((), ())), preferred_element_type=F32
        ).astype(BF16)
    for q in range(n_d):
        start = pl.multiple_of((d ^ q) * rows, 16)
        at_ref[q * rows : (q + 1) * rows, :] = held[pl.ds(start, rows), :]
    tok = jnp.concatenate([r[0:tokens, :] for r in firsts], axis=0)
    prod = jnp.dot(at_ref[...], tok, preferred_element_type=F32)
    _split(prod, keep_blocks, send_blocks, rows, keep_ref, send_ref)


def _partial_kernel(n_e, keep_blocks, send_blocks, rows, at_ref, *refs):
    tok = jnp.concatenate([r[...] for r in refs[:n_e]], axis=0)
    prod = jnp.dot(at_ref[...], tok, preferred_element_type=F32)
    _split(prod, keep_blocks, send_blocks, rows, *refs[n_e:])


def _slot_kernel(n_e, hidden, where_ref, pre_ref, w_ref, after_ref, *refs):
    firsts, rests, (pre_grad_ref, back_ref, rows_ref) = refs[:n_e], refs[n_e : 2 * n_e], refs[2 * n_e :]
    e = where_ref[1]
    expert = e.astype(F32)
    capacity = pre_ref.shape[1]
    tokens = rests[0].shape[0]
    picks, weights = [], []
    for j in range(n_e):
        chosen, slot_weight = _choice(_info(firsts[j], tokens), expert, capacity)
        picks.append(chosen)
        weights.append(slot_weight)
        pick = chosen.astype(BF16)
        here = slice(j * capacity, (j + 1) * capacity)
        rows_ref[here, :TILE] = jnp.dot(
            pick, firsts[j][0:tokens, :], preferred_element_type=F32
        ).astype(BF16)
        rows_ref[here, TILE:] = jnp.dot(pick, rests[j][...], preferred_element_type=F32).astype(BF16)
    tile = 256 if hidden % 256 == 0 else hidden
    gates = [jnp.zeros((capacity, 1), F32) for _ in range(n_e)]
    for h in range(0, hidden, tile):
        raw_all = lax.dot_general(
            rows_ref[...], w_ref[0, h : h + tile, :], (((1,), (1,)), ((), ())), preferred_element_type=F32
        )
        for j in range(n_e):
            raw = raw_all[j * capacity : (j + 1) * capacity, :]
            a = pre_ref[e ^ j, :, h : h + tile].astype(F32)
            u = pre_ref[e ^ j, :, hidden + h : hidden + h + tile].astype(F32)
            s = jax.nn.sigmoid(a)
            silu = a * s
            gates[j] = gates[j] + jnp.sum(silu * u * raw, axis=1, keepdims=True)
            delta = weights[j] * raw
            pre_grad_ref[e ^ j, :, h : h + tile] = (delta * u * s * (1.0 + a * (1.0 - s))).astype(BF16)
            pre_grad_ref[e ^ j, :, hidden + h : hidden + h + tile] = (delta * silu).astype(BF16)
    for j in range(n_e):
        back_ref[e ^ j] = jnp.sum(picks[j] * gates[j], axis=0, keepdims=True)


VM = pl.BlockSpec(memory_space=pltpu.VMEM)
SM = pl.BlockSpec(memory_space=pltpu.SMEM)
ANY = pl.BlockSpec(memory_space=pl.ANY)


def _call(body, name, outs, in_specs, out_specs, mib, flops=0, scratch=(), **more):
    return pl.pallas_call(
        body,
        out_shape=outs,
        in_specs=in_specs,
        out_specs=out_specs,
        scratch_shapes=scratch,
        compiler_params=pltpu.CompilerParams(vmem_limit_bytes=mib * MIB),
        cost_estimate=pl.CostEstimate(flops=flops, bytes_accessed=4 * MIB, transcendentals=0),
        name=name,
        **more,
    )


def _shape(shape, dtype):
    return jax.ShapeDtypeStruct(shape, dtype)


def _fast(grad_tokens, routes, combine, down_weight, saved_pre):
    n_d, n_e = lax.axis_size("dp"), lax.axis_size("expert")
    tokens, width = grad_tokens.shape
    hidden = down_weight.shape[1]
    capacity = saved_pre.shape[3]
    rows = hidden // n_d
    depth = n_e * tokens
    where = jnp.stack([lax.axis_index("dp"), lax.axis_index("expert")]).astype(jnp.int32)
    pre = saved_pre.reshape(saved_pre.shape[1:])[0]

    first, rest = _call(
        functools.partial(_pack_kernel, tokens),
        "pack_tokens",
        (_shape((tokens + INFO_ROWS, TILE), BF16), _shape((tokens, width - TILE), BF16)),
        [VM] * 3,
        (VM, VM),
        8,
    )(routes.T, combine.T, grad_tokens)

    def gather(block):
        held = {0: block}
        for bit in reversed(range(n_e.bit_length() - 1)):
            for key in sorted(held):
                held[key | (1 << bit)] = _send(held[key], 0, 1 << bit)
        return [held[j] for j in range(n_e)]

    firsts = gather(first)
    rests = gather(rest)

    act = _call(
        functools.partial(_activate_kernel, hidden),
        "activation",
        _shape((n_e, capacity, hidden), F32),
        [VM],
        VM,
        12,
    )(pre)

    last = tuple(range(2, n_d.bit_length() - 1))
    orders = {"x": ((0,), (1,), last), "z": ((1,), last, (0,))}

    def blocks_of(stages):
        blocks = [0]
        for b in [b for group in stages for b in group]:
            blocks = [q | (v << b) for q in blocks for v in (0, 1)]
        kept = len(blocks) >> len(stages[0])
        return tuple(blocks[:kept]), tuple(blocks[kept:])

    def parts_of(kept, sent):
        return (
            _shape((len(kept) * rows, TILE), F32),
            _shape((len(sent) * rows, TILE), BF16),
        )

    state = []
    stages = orders[ORDERS[0]]
    kept, sent = blocks_of(stages)
    at_all, keep, send = _call(
        functools.partial(_first_kernel, n_e, n_d, kept, sent),
        "first_partial",
        (_shape((hidden, depth), BF16),) + parts_of(kept, sent),
        [SM] + [VM] * (1 + n_e),
        (VM, VM, VM),
        16,
        2 * hidden * depth * TILE,
        [pltpu.VMEM((hidden, depth), BF16)],
    )(where, act, *firsts)
    state.append([stages, keep, send])
    for c in range(1, width // TILE):
        stages = orders[ORDERS[c % len(ORDERS)]]
        kept, sent = blocks_of(stages)
        outs = parts_of(kept, sent)
        keep, send = _call(
            functools.partial(_partial_kernel, n_e, kept, sent, rows),
            "partial_chunk",
            outs,
            [pl.BlockSpec((hidden, depth), lambda i: (0, 0))]
            + [pl.BlockSpec((tokens, TILE), lambda i, c=c: (0, c - 1))] * n_e,
            tuple(pl.BlockSpec(o.shape, lambda i: (0, 0)) for o in outs),
            16,
            2 * hidden * depth * TILE,
            grid=(1,),
        )(at_all, *rests)
        state.append([stages, keep, send])

    pre_grad, back = _call(
        functools.partial(_slot_kernel, n_e, hidden),
        "slot_gradients",
        (_shape(pre.shape, BF16), _shape((n_e, 1, tokens), F32)),
        [SM, VM, VM, ANY] + [VM] * (2 * n_e),
        (VM, VM),
        24,
        2 * n_e * capacity * width * hidden,
        [pltpu.VMEM((n_e * capacity, width), BF16)],
    )(where, pre, down_weight, state[-1][1], *firsts, *rests)

    finals = [None] * len(state)
    for s in range(3):
        for c, (stages, keep, send) in enumerate(state):
            group = stages[s]
            size = keep.shape[0]
            total = keep
            for v in range(1, 1 << len(group)):
                mask = sum((1 << b) for i, b in enumerate(group) if (v >> (len(group) - 1 - i)) & 1)
                got = _send(send[(v - 1) * size : v * size], mask, 0)
                total = total + got.astype(F32)
            if s < 2:
                size >>= len(stages[s + 1])
                state[c][1], state[c][2] = total[:size], total[size:].astype(BF16)
            else:
                finals[c] = total * (1.0 / n_d)
    down_grad = jnp.concatenate(finals, axis=1).reshape(1, rows * width)

    returned = lax.all_to_all(back, "expert", split_axis=0, concat_axis=0, tiled=True)
    gate_grad = sum(jnp.where(routes.T == k, returned[k], 0.0) for k in range(n_e)).T
    return pre_grad.reshape(saved_pre.shape), down_grad, gate_grad


def _general(grad_tokens, routes, combine, down_weight, saved_pre):
    experts = lax.axis_size("expert")
    tok_rows, route_count = routes.shape
    capacity = saved_pre.shape[3]
    model_width = grad_tokens.shape[1]
    hidden = down_weight.shape[1]
    flat_routes = routes.reshape(-1)
    onehot = (flat_routes[:, None] == jnp.arange(experts, dtype=jnp.int32)[None, :]).astype(jnp.int32)
    before = jnp.cumsum(onehot, axis=0) - onehot
    position = jnp.sum(before * onehot, axis=1)
    slot_id = flat_routes * capacity + position
    slot_grid = jnp.arange(experts * capacity, dtype=jnp.int32)
    chosen = slot_grid[:, None] == slot_id[None, :]
    placing = jnp.any(chosen.reshape(experts * capacity, tok_rows, route_count), axis=2).astype(BF16)
    outgoing = jnp.dot(placing, grad_tokens, preferred_element_type=F32).astype(BF16)
    combine_flat = combine.reshape(-1).astype(F32)
    out_weight = jnp.sum(jnp.where(chosen, combine_flat[None, :], 0.0), axis=1).astype(BF16)
    swap = functools.partial(lax.all_to_all, axis_name="expert", split_axis=0, concat_axis=0, tiled=True)
    slot_rows = swap(outgoing.reshape(experts, capacity, model_width)).reshape(-1, model_width)
    slot_weight = swap(out_weight.reshape(experts, capacity)).reshape(-1).astype(F32)
    raw_grad = lax.dot_general(
        slot_rows, down_weight[0], (((1,), (1,)), ((), ())), preferred_element_type=F32
    )
    pre_acts = saved_pre.reshape(-1, 2 * hidden).astype(F32)
    gate_pre, up_pre = pre_acts[:, :hidden], pre_acts[:, hidden:]
    logistic = jax.nn.sigmoid(gate_pre)
    activated = gate_pre * logistic
    hidden_act = activated * up_pre
    slot_gate = jnp.sum(hidden_act * raw_grad, axis=1)
    hidden_delta = slot_weight[:, None] * raw_grad
    gate_delta = hidden_delta * up_pre * logistic * (1.0 + gate_pre * (1.0 - logistic))
    pre_grad = jnp.concatenate([gate_delta, hidden_delta * activated], axis=1).astype(BF16)
    scaled = (slot_weight[:, None] * hidden_act).astype(BF16)
    whole_term = lax.dot_general(
        scaled, slot_rows, (((0,), (0,)), ((), ())), preferred_element_type=F32
    )
    summed = lax.psum_scatter(whole_term.reshape(-1), "dp", scatter_dimension=0, tiled=True)
    down_grad = (summed / lax.axis_size("dp"))[None]
    returned_flat = swap(slot_gate.reshape(experts, capacity)).reshape(-1)
    gate_flat = jnp.sum(jnp.where(chosen, returned_flat[:, None], 0.0), axis=0)
    return pre_grad.reshape(saved_pre.shape), down_grad, gate_flat.reshape(tok_rows, route_count)


def solution(mesh):
    n_d, n_e = mesh.shape["dp"], mesh.shape["expert"]

    def per_device(grad_tokens, routes, combine, down_weight, saved_pre):
        hidden, width = down_weight.shape[1:]
        whole_tiles = (
            hidden % (16 * n_d) == 0
            and saved_pre.shape[3] % 16 == 0
            and width % TILE == 0
            and grad_tokens.shape[0] == 128
            and n_d >= 8
            and n_d & (n_d - 1) == 0
            and n_e >= 2
            and n_e & (n_e - 1) == 0
            and routes.shape[1] == 2
        )
        form = _fast if whole_tiles else _general
        return form(grad_tokens, routes, combine, down_weight, saved_pre)

    by_both = P(("dp", "expert"), None)
    by_expert = P("expert", "dp", None, None, None)
    return jax.shard_map(
        per_device,
        mesh=mesh,
        in_specs=(by_both, by_both, by_both, P("expert", None, None), by_expert),
        out_specs=(by_expert, P("expert", "dp"), by_both),
        check_vma=False,
    )
```

```python
import functools

import jax
import jax.numpy as jnp
from jax import lax
from jax.experimental import pallas as pl
from jax.experimental.pallas import tpu as pltpu
from jax.sharding import PartitionSpec as P

F32 = jnp.float32
BF16 = jnp.bfloat16
AXES = ("dp", "expert")
MIB = 1024 * 1024
INFO_ROWS = 16
PACK_MIB = 60
EIGHTHS = (3, 2, 2, 1)


def _send(value, dp_mask, expert_mask):
    dps, experts = lax.axis_size("dp"), lax.axis_size("expert")
    pairs = [
        (d * experts + e, (d ^ dp_mask) * experts + (e ^ expert_mask))
        for d in range(dps)
        for e in range(experts)
    ]
    return lax.ppermute(value, AXES, pairs)


def _choice(info, expert, capacity):
    tokens = info.shape[1]
    first, second = info[0:1, :] == expert, info[1:2, :] == expert
    named = jnp.where(first | second, 1.0, 0.0)
    weight = jnp.where(first, info[2:3, :], 0.0) + jnp.where(second, info[3:4, :], 0.0)
    row = lax.broadcasted_iota(jnp.int32, (tokens, tokens), 0)
    col = lax.broadcasted_iota(jnp.int32, (tokens, tokens), 1)
    earlier = jnp.where(row < col, 1.0, 0.0).astype(BF16)
    position = jnp.dot(
        jnp.broadcast_to(named, (8, tokens)).astype(BF16), earlier, preferred_element_type=F32
    )[0:1, :]
    slot = lax.broadcasted_iota(jnp.int32, (capacity, tokens), 0).astype(F32)
    chosen = jnp.where((slot == position) & (named > 0.0), 1.0, 0.0)
    slot_weight = jnp.sum(chosen * weight, axis=1, keepdims=True)
    return chosen, slot_weight


def _pack_kernel(tokens, lead, routes_ref, combine_ref, tok_ref, first_ref, rest_ref):
    first_ref[0:tokens, :] = tok_ref[:, :lead]
    first_ref[tokens:, :] = jnp.zeros((INFO_ROWS, lead), BF16)
    info = jnp.concatenate(
        [
            routes_ref[...].astype(F32),
            combine_ref[...].astype(F32),
            jnp.zeros((INFO_ROWS - 4, tokens), F32),
        ],
        axis=0,
    )
    first_ref[tokens:, 0:tokens] = info.astype(BF16)
    rest_ref[...] = tok_ref[:, lead:]


def _activate_kernel(hidden, pre_ref, out_ref):
    for j in range(pre_ref.shape[0]):
        pre = pre_ref[j].astype(F32)
        gate, up = pre[:, :hidden], pre[:, hidden:]
        out_ref[j] = gate * jax.nn.sigmoid(gate) * up


def _info(ref, tokens):
    return ref[tokens : tokens + INFO_ROWS, 0:tokens].astype(F32)


def _split(prod, keep_blocks, send_blocks, rows, keep_ref, send_ref):
    for p, q in enumerate(keep_blocks):
        keep_ref[p * rows : (p + 1) * rows, :] = prod[q * rows : (q + 1) * rows, :]
    for p, q in enumerate(send_blocks):
        send_ref[p * rows : (p + 1) * rows, :] = prod[q * rows : (q + 1) * rows, :].astype(BF16)


def _first_kernel(n_e, n_d, keep_blocks, send_blocks, where_ref, act_ref, *refs):
    firsts, (at_ref, keep_ref, send_ref, held) = refs[:n_e], refs[n_e:]
    d, e = where_ref[0], where_ref[1]
    expert = e.astype(F32)
    capacity, hidden = act_ref.shape[1:]
    tokens = firsts[0].shape[0] - INFO_ROWS
    rows = hidden // n_d
    for j in range(n_e):
        chosen, slot_weight = _choice(_info(firsts[j], tokens), expert, capacity)
        scaled = (slot_weight * act_ref[e ^ j]).astype(BF16)
        held[:, j * tokens : (j + 1) * tokens] = lax.dot_general(
            scaled, chosen.astype(BF16), (((0,), (0,)), ((), ())), preferred_element_type=F32
        ).astype(BF16)
    for q in range(n_d):
        start = pl.multiple_of((d ^ q) * rows, 16)
        at_ref[q * rows : (q + 1) * rows, :] = held[pl.ds(start, rows), :]
    tok = jnp.concatenate([r[0:tokens, :] for r in firsts], axis=0)
    prod = jnp.dot(at_ref[...], tok, preferred_element_type=F32)
    _split(prod, keep_blocks, send_blocks, rows, keep_ref, send_ref)


def _partial_kernel(n_e, keep_blocks, send_blocks, rows, columns, at_ref, *refs):
    tok = jnp.concatenate([r[:, columns] for r in refs[:n_e]], axis=0)
    prod = jnp.dot(at_ref[...], tok, preferred_element_type=F32)
    _split(prod, keep_blocks, send_blocks, rows, *refs[n_e:])


def _slot_kernel(n_e, hidden, where_ref, pre_ref, w_ref, *refs):
    firsts, rests, (pre_grad_ref, back_ref, rows_ref) = refs[:n_e], refs[n_e : 2 * n_e], refs[2 * n_e :]
    e = where_ref[1]
    expert = e.astype(F32)
    capacity = pre_ref.shape[1]
    tokens = rests[0].shape[0]
    lead = firsts[0].shape[1]
    picks, weights = [], []
    for j in range(n_e):
        chosen, slot_weight = _choice(_info(firsts[j], tokens), expert, capacity)
        picks.append(chosen)
        weights.append(slot_weight)
        pick = chosen.astype(BF16)
        here = slice(j * capacity, (j + 1) * capacity)
        rows_ref[here, :lead] = jnp.dot(
            pick, firsts[j][0:tokens, :], preferred_element_type=F32
        ).astype(BF16)
        rows_ref[here, lead:] = jnp.dot(pick, rests[j][...], preferred_element_type=F32).astype(BF16)
    tile = 256 if hidden % 256 == 0 else hidden
    gates = [jnp.zeros((capacity, 1), F32) for _ in range(n_e)]
    for h in range(0, hidden, tile):
        raw_all = lax.dot_general(
            rows_ref[...], w_ref[0, h : h + tile, :], (((1,), (1,)), ((), ())), preferred_element_type=F32
        )
        for j in range(n_e):
            raw = raw_all[j * capacity : (j + 1) * capacity, :]
            a = pre_ref[e ^ j, :, h : h + tile].astype(F32)
            u = pre_ref[e ^ j, :, hidden + h : hidden + h + tile].astype(F32)
            s = jax.nn.sigmoid(a)
            silu = a * s
            gates[j] = gates[j] + jnp.sum(silu * u * raw, axis=1, keepdims=True)
            delta = weights[j] * raw
            pre_grad_ref[e ^ j, :, h : h + tile] = (delta * u * s * (1.0 + a * (1.0 - s))).astype(BF16)
            pre_grad_ref[e ^ j, :, hidden + h : hidden + h + tile] = (delta * silu).astype(BF16)
    for j in range(n_e):
        back_ref[e ^ j] = jnp.sum(picks[j] * gates[j], axis=0, keepdims=True)


def _sum_kernel(keep_ref, got_ref, next_keep_ref, next_send_ref):
    size = next_keep_ref.shape[0]
    next_keep_ref[...] = keep_ref[0:size, :] + got_ref[0:size, :].astype(F32)
    next_send_ref[...] = (keep_ref[size:, :] + got_ref[size:, :].astype(F32)).astype(BF16)


def _finish_kernel(scale, counts, *refs):
    parts, out_ref = refs[:-1], refs[-1]
    rows = parts[0].shape[0]
    lanes = out_ref.shape[0] // rows
    at = 0
    for count in counts:
        total = parts[0][...]
        for more in parts[1:count]:
            total = total + more[...].astype(F32)
        parts = parts[count:]
        total = total * scale
        for j in range(0, total.shape[1], 128):
            out_ref[pl.ds(at, rows, stride=lanes), :] = total[:, j : j + 128]
            at += 1


def _after(value, *others):
    return lax.optimization_barrier((value,) + others)[0]


VM = pl.BlockSpec(memory_space=pltpu.VMEM)
SM = pl.BlockSpec(memory_space=pltpu.SMEM)


def _call(body, name, outs, in_specs, out_specs, mib, flops=0, scratch=(), **more):
    return pl.pallas_call(
        body,
        out_shape=outs,
        in_specs=in_specs,
        out_specs=out_specs,
        scratch_shapes=scratch,
        compiler_params=pltpu.CompilerParams(vmem_limit_bytes=mib * MIB),
        cost_estimate=pl.CostEstimate(flops=flops, bytes_accessed=4 * MIB, transcendentals=0),
        name=name,
        **more,
    )


def _shape(shape, dtype):
    return jax.ShapeDtypeStruct(shape, dtype)


def _fast(grad_tokens, routes, combine, down_weight, saved_pre):
    n_d, n_e = lax.axis_size("dp"), lax.axis_size("expert")
    tokens, width = grad_tokens.shape
    hidden = down_weight.shape[1]
    capacity = saved_pre.shape[3]
    rows = hidden // n_d
    depth = n_e * tokens
    lanes = width // 128
    where = jnp.stack([lax.axis_index("dp"), lax.axis_index("expert")]).astype(jnp.int32)
    pre = saved_pre.reshape(saved_pre.shape[1:])[0]
    sizes = [part * width // 8 for part in EIGHTHS]
    lead = sizes[0]

    first, rest = _call(
        functools.partial(_pack_kernel, tokens, lead),
        "pack_tokens",
        (_shape((tokens + INFO_ROWS, lead), BF16), _shape((tokens, width - lead), BF16)),
        [VM] * 3,
        (VM, VM),
        PACK_MIB,
    )(routes.T, combine.T, grad_tokens)

    def gather(block, *later):
        held = {0: block}
        for bit in reversed(range(n_e.bit_length() - 1)):
            for key in sorted(held):
                value = _after(held[key], *later) if later and bit == 0 else held[key]
                held[key | (1 << bit)] = _send(value, 0, 1 << bit)
        return [held[j] for j in range(n_e)]

    firsts = gather(first)

    act = _call(
        functools.partial(_activate_kernel, hidden),
        "activation",
        _shape((n_e, capacity, hidden), F32),
        [VM],
        VM,
        12,
    )(pre)

    last = tuple(range(2, n_d.bit_length() - 1))
    by_x, by_z, at_once = ((0,), (1,), last), ((1,), last, (0,)), ((0,), (1,) + last)

    def blocks_of(stages):
        blocks = [0]
        for b in [b for group in stages for b in group]:
            blocks = [q | (v << b) for q in blocks for v in (0, 1)]
        kept = len(blocks) >> len(stages[0])
        return tuple(blocks[:kept]), tuple(blocks[kept:])

    def halves(kept, sent, size):
        return _shape((kept * rows, size), F32), _shape((sent * rows, size), BF16)

    def exchange(send, size, group):
        got = []
        for v in range(1, 1 << len(group)):
            mask = sum((1 << b) for i, b in enumerate(group) if (v >> (len(group) - 1 - i)) & 1)
            got.append(_send(send[(v - 1) * size : v * size], mask, 0))
        return got

    def merge(keep, got):
        for more in got[:-1]:
            keep = keep + more.astype(F32)
        return keep, got[-1]

    def add(keep, got, group):
        keep, got = merge(keep, got)
        size = keep.shape[0] // rows
        kept = size >> len(group)
        return _call(
            _sum_kernel,
            "sum_halves",
            halves(kept, size - kept, keep.shape[1]),
            [VM, VM],
            (VM, VM),
            8,
        )(keep, got)

    kept, sent = blocks_of(by_x)
    at_all, keep_a, send_a = _call(
        functools.partial(_first_kernel, n_e, n_d, kept, sent),
        "first_partial",
        (_shape((hidden, depth), BF16),) + halves(len(kept), len(sent), lead),
        [SM] + [VM] * (1 + n_e),
        (VM, VM, VM),
        16,
        2 * hidden * depth * lead,
        [pltpu.VMEM((hidden, depth), BF16)],
    )(where, act, *firsts)
    got_a = exchange(send_a, keep_a.shape[0], by_x[0])

    rests = gather(_after(rest, firsts[n_e // 2]), send_a)
    rests[0] = rest

    def partial(chunk, stages):
        kept, sent = blocks_of(stages)
        start = sum(sizes[1:chunk])
        columns = slice(start, start + sizes[chunk])
        return _call(
            functools.partial(_partial_kernel, n_e, kept, sent, rows, columns),
            "partial_chunk",
            halves(len(kept), len(sent), sizes[chunk]),
            [VM] * (1 + n_e),
            (VM, VM),
            16,
            2 * hidden * depth * sizes[chunk],
        )(at_all, *rests)

    keep_b, send_b = partial(1, by_x)
    keep_c, send_c = partial(2, at_once)
    keep_z, send_z = partial(3, by_z)

    got_z = exchange(send_z, keep_z.shape[0], by_z[0])
    pre_grad, back = _call(
        functools.partial(_slot_kernel, n_e, hidden),
        "slot_gradients",
        (_shape(pre.shape, BF16), _shape((n_e, 1, tokens), F32)),
        [SM] + [VM] * (2 + 2 * n_e),
        (VM, VM),
        24,
        2 * n_e * capacity * width * hidden,
        [pltpu.VMEM((n_e * capacity, width), BF16)],
    )(_after(where, send_b, send_c, send_z), pre, down_weight, *firsts, *rests)
    returned = lax.all_to_all(back, "expert", split_axis=0, concat_axis=0, tiled=True)

    got_b = exchange(_after(send_b, back, *got_a), keep_b.shape[0], by_x[0])
    keep_a, send_a = add(_after(keep_a, back, send_z), got_a, by_x[1])
    got_a = exchange(send_a, keep_a.shape[0], by_x[1])

    got_c = exchange(_after(send_c, returned, *got_b, *got_z, *got_a), keep_c.shape[0], at_once[0])
    keep_b, send_b = add(keep_b, got_b, by_x[1])
    got_b = exchange(send_b, keep_b.shape[0], by_x[1])
    keep_z, send_z = add(keep_z, got_z, by_z[1])
    got_z = exchange(send_z, keep_z.shape[0], by_z[1])
    keep_a, send_a = add(keep_a, got_a, by_x[2])
    end_a = [keep_a] + exchange(send_a, keep_a.shape[0], by_x[2])

    keep_c, send_c = add(_after(keep_c, *got_z, *got_b, end_a[1]), got_c, at_once[1])
    end_c = [keep_c] + exchange(send_c, keep_c.shape[0], at_once[1])
    keep_b, send_b = add(keep_b, got_b, by_x[2])
    end_b = [keep_b] + exchange(send_b, keep_b.shape[0], by_x[2])
    keep_z, send_z = add(keep_z, got_z, by_z[2])
    end_z = [keep_z] + exchange(send_z, keep_z.shape[0], by_z[2])

    ends = (end_a, end_b, end_c, end_z)
    down_grad = _call(
        functools.partial(_finish_kernel, 1.0 / n_d, tuple(len(end) for end in ends)),
        "finish",
        _shape((rows * lanes, 128), F32),
        [VM] * sum(len(end) for end in ends),
        VM,
        8,
    )(*[part for end in ends for part in end]).reshape(1, rows * width)

    gate_grad = sum(jnp.where(routes.T == k, returned[k], 0.0) for k in range(n_e)).T
    return pre_grad.reshape(saved_pre.shape), down_grad, gate_grad


def _general(grad_tokens, routes, combine, down_weight, saved_pre):
    experts = lax.axis_size("expert")
    tok_rows, route_count = routes.shape
    capacity = saved_pre.shape[3]
    model_width = grad_tokens.shape[1]
    hidden = down_weight.shape[1]
    flat_routes = routes.reshape(-1)
    onehot = (flat_routes[:, None] == jnp.arange(experts, dtype=jnp.int32)[None, :]).astype(jnp.int32)
    before = jnp.cumsum(onehot, axis=0) - onehot
    position = jnp.sum(before * onehot, axis=1)
    slot_id = flat_routes * capacity + position
    slot_grid = jnp.arange(experts * capacity, dtype=jnp.int32)
    chosen = slot_grid[:, None] == slot_id[None, :]
    placing = jnp.any(chosen.reshape(experts * capacity, tok_rows, route_count), axis=2).astype(BF16)
    outgoing = jnp.dot(placing, grad_tokens, preferred_element_type=F32).astype(BF16)
    combine_flat = combine.reshape(-1).astype(F32)
    out_weight = jnp.sum(jnp.where(chosen, combine_flat[None, :], 0.0), axis=1).astype(BF16)
    swap = functools.partial(lax.all_to_all, axis_name="expert", split_axis=0, concat_axis=0, tiled=True)
    slot_rows = swap(outgoing.reshape(experts, capacity, model_width)).reshape(-1, model_width)
    slot_weight = swap(out_weight.reshape(experts, capacity)).reshape(-1).astype(F32)
    raw_grad = lax.dot_general(
        slot_rows, down_weight[0], (((1,), (1,)), ((), ())), preferred_element_type=F32
    )
    pre_acts = saved_pre.reshape(-1, 2 * hidden).astype(F32)
    gate_pre, up_pre = pre_acts[:, :hidden], pre_acts[:, hidden:]
    logistic = jax.nn.sigmoid(gate_pre)
    activated = gate_pre * logistic
    hidden_act = activated * up_pre
    slot_gate = jnp.sum(hidden_act * raw_grad, axis=1)
    hidden_delta = slot_weight[:, None] * raw_grad
    gate_delta = hidden_delta * up_pre * logistic * (1.0 + gate_pre * (1.0 - logistic))
    pre_grad = jnp.concatenate([gate_delta, hidden_delta * activated], axis=1).astype(BF16)
    scaled = (slot_weight[:, None] * hidden_act).astype(BF16)
    whole_term = lax.dot_general(
        scaled, slot_rows, (((0,), (0,)), ((), ())), preferred_element_type=F32
    )
    summed = lax.psum_scatter(whole_term.reshape(-1), "dp", scatter_dimension=0, tiled=True)
    down_grad = (summed / lax.axis_size("dp"))[None]
    returned_flat = swap(slot_gate.reshape(experts, capacity)).reshape(-1)
    gate_flat = jnp.sum(jnp.where(chosen, returned_flat[:, None], 0.0), axis=0)
    return pre_grad.reshape(saved_pre.shape), down_grad, gate_flat.reshape(tok_rows, route_count)


def solution(mesh):
    n_d, n_e = mesh.shape["dp"], mesh.shape["expert"]

    def per_device(grad_tokens, routes, combine, down_weight, saved_pre):
        hidden, width = down_weight.shape[1:]
        whole_tiles = (
            hidden % (16 * n_d) == 0
            and saved_pre.shape[3] % 16 == 0
            and width % 1024 == 0
            and grad_tokens.shape[0] == 128
            and n_d >= 8
            and n_d & (n_d - 1) == 0
            and n_e >= 2
            and n_e & (n_e - 1) == 0
            and routes.shape[1] == 2
        )
        form = _fast if whole_tiles else _general
        return form(grad_tokens, routes, combine, down_weight, saved_pre)

    by_both = P(("dp", "expert"), None)
    by_expert = P("expert", "dp", None, None, None)
    return jax.shard_map(
        per_device,
        mesh=mesh,
        in_specs=(by_both, by_both, by_both, P("expert", None, None), by_expert),
        out_specs=(by_expert, P("expert", "dp"), by_both),
        check_vma=False,
    )
```

```python
import functools

import jax
import jax.numpy as jnp
from jax import lax
from jax.experimental import pallas as pl
from jax.experimental.pallas import tpu as pltpu
from jax.sharding import PartitionSpec as P

F32 = jnp.float32
BF16 = jnp.bfloat16
AXES = ("dp", "expert")
MIB = 1024 * 1024
INFO_ROWS = 16
PACK_MIB = 60
LEAD_FLOPS = 6 * 10**9
SIXTEENTHS = (6, 5, 3, 2)


def _send(value, dp_mask, expert_mask):
    dps, experts = lax.axis_size("dp"), lax.axis_size("expert")
    pairs = [
        (d * experts + e, (d ^ dp_mask) * experts + (e ^ expert_mask))
        for d in range(dps)
        for e in range(experts)
    ]
    return lax.ppermute(value, AXES, pairs)


def _choice(info, expert, capacity):
    tokens = info.shape[1]
    first, second = info[0:1, :] == expert, info[1:2, :] == expert
    named = jnp.where(first | second, 1.0, 0.0)
    weight = jnp.where(first, info[2:3, :], 0.0) + jnp.where(second, info[3:4, :], 0.0)
    row = lax.broadcasted_iota(jnp.int32, (tokens, tokens), 0)
    col = lax.broadcasted_iota(jnp.int32, (tokens, tokens), 1)
    earlier = jnp.where(row < col, 1.0, 0.0).astype(BF16)
    position = jnp.dot(
        jnp.broadcast_to(named, (8, tokens)).astype(BF16), earlier, preferred_element_type=F32
    )[0:1, :]
    slot = lax.broadcasted_iota(jnp.int32, (capacity, tokens), 0).astype(F32)
    chosen = jnp.where((slot == position) & (named > 0.0), 1.0, 0.0)
    slot_weight = jnp.sum(chosen * weight, axis=1, keepdims=True)
    return chosen, slot_weight


def _pack_kernel(tokens, lead, routes_ref, combine_ref, tok_ref, first_ref):
    first_ref[0:tokens, :] = tok_ref[...]
    first_ref[tokens:, :] = jnp.zeros((INFO_ROWS, lead), BF16)
    info = jnp.concatenate(
        [
            routes_ref[...].astype(F32),
            combine_ref[...].astype(F32),
            jnp.zeros((INFO_ROWS - 4, tokens), F32),
        ],
        axis=0,
    )
    first_ref[tokens:, 0:tokens] = info.astype(BF16)


def _activate_kernel(hidden, pre_ref, out_ref):
    for j in range(pre_ref.shape[0]):
        pre = pre_ref[j].astype(F32)
        gate, up = pre[:, :hidden], pre[:, hidden:]
        out_ref[j] = gate * jax.nn.sigmoid(gate) * up


def _info(ref, tokens):
    return ref[tokens : tokens + INFO_ROWS, 0:tokens].astype(F32)


def _split(prod, keep_blocks, send_blocks, rows, keep_ref, send_ref):
    for p, q in enumerate(keep_blocks):
        keep_ref[p * rows : (p + 1) * rows, :] = prod[q * rows : (q + 1) * rows, :]
    for p, q in enumerate(send_blocks):
        send_ref[p * rows : (p + 1) * rows, :] = prod[q * rows : (q + 1) * rows, :].astype(BF16)


def _first_kernel(n_e, n_d, keep_blocks, send_blocks, where_ref, act_ref, *refs):
    firsts, (at_ref, keep_ref, send_ref, held) = refs[:n_e], refs[n_e:]
    d, e = where_ref[0], where_ref[1]
    expert = e.astype(F32)
    capacity, hidden = act_ref.shape[1:]
    tokens = firsts[0].shape[0] - INFO_ROWS
    rows = hidden // n_d
    for j in range(n_e):
        chosen, slot_weight = _choice(_info(firsts[j], tokens), expert, capacity)
        scaled = (slot_weight * act_ref[e ^ j]).astype(BF16)
        held[:, j * tokens : (j + 1) * tokens] = lax.dot_general(
            scaled, chosen.astype(BF16), (((0,), (0,)), ((), ())), preferred_element_type=F32
        ).astype(BF16)
    for q in range(n_d):
        start = pl.multiple_of((d ^ q) * rows, 16)
        at_ref[q * rows : (q + 1) * rows, :] = held[pl.ds(start, rows), :]
    tok = jnp.concatenate([r[0:tokens, :] for r in firsts], axis=0)
    prod = jnp.dot(at_ref[...], tok, preferred_element_type=F32)
    _split(prod, keep_blocks, send_blocks, rows, keep_ref, send_ref)


def _partial_kernel(n_e, keep_blocks, send_blocks, rows, columns, at_ref, *refs):
    tok = jnp.concatenate([r[:, columns] for r in refs[:n_e]], axis=0)
    prod = jnp.dot(at_ref[...], tok, preferred_element_type=F32)
    _split(prod, keep_blocks, send_blocks, rows, *refs[n_e:])


def _lead_kernel(n_e, capacity, where_ref, w_ref, *refs):
    firsts, raw_ref, rows_ref = refs[:n_e], refs[n_e], refs[n_e + 1]
    expert = where_ref[1].astype(F32)
    lead = firsts[0].shape[1]
    tokens = firsts[0].shape[0] - INFO_ROWS
    for j in range(n_e):
        chosen, _ = _choice(_info(firsts[j], tokens), expert, capacity)
        rows_ref[j * capacity : (j + 1) * capacity, :] = jnp.dot(
            chosen.astype(BF16), firsts[j][0:tokens, :], preferred_element_type=F32
        ).astype(BF16)
    raw_ref[...] = lax.dot_general(
        rows_ref[...], w_ref[0, :, 0:lead], (((1,), (1,)), ((), ())), preferred_element_type=F32
    )


def _slot_kernel(n_e, hidden, where_ref, pre_ref, w_ref, raw_ref, *refs):
    infos, rests, (pre_grad_ref, back_ref, rows_ref) = refs[:n_e], refs[n_e : 2 * n_e], refs[2 * n_e :]
    e = where_ref[1]
    expert = e.astype(F32)
    capacity = pre_ref.shape[1]
    tokens = rests[0].shape[0]
    lead = infos[0].shape[1]
    picks, weights = [], []
    for j in range(n_e):
        chosen, slot_weight = _choice(_info(infos[j], tokens), expert, capacity)
        picks.append(chosen)
        weights.append(slot_weight)
        rows_ref[j * capacity : (j + 1) * capacity, :] = jnp.dot(
            chosen.astype(BF16), rests[j][...], preferred_element_type=F32
        ).astype(BF16)
    tile = 256 if hidden % 256 == 0 else hidden
    gates = [jnp.zeros((capacity, 1), F32) for _ in range(n_e)]
    for h in range(0, hidden, tile):
        raw_all = raw_ref[:, h : h + tile] + lax.dot_general(
            rows_ref[...],
            w_ref[0, h : h + tile, lead:],
            (((1,), (1,)), ((), ())),
            preferred_element_type=F32,
        )
        for j in range(n_e):
            raw = raw_all[j * capacity : (j + 1) * capacity, :]
            a = pre_ref[e ^ j, :, h : h + tile].astype(F32)
            u = pre_ref[e ^ j, :, hidden + h : hidden + h + tile].astype(F32)
            s = jax.nn.sigmoid(a)
            silu = a * s
            gates[j] = gates[j] + jnp.sum(silu * u * raw, axis=1, keepdims=True)
            delta = weights[j] * raw
            pre_grad_ref[e ^ j, :, h : h + tile] = (delta * u * s * (1.0 + a * (1.0 - s))).astype(BF16)
            pre_grad_ref[e ^ j, :, hidden + h : hidden + h + tile] = (delta * silu).astype(BF16)
    for j in range(n_e):
        back_ref[e ^ j] = jnp.sum(picks[j] * gates[j], axis=0, keepdims=True)


def _sum_kernel(keep_ref, got_ref, next_keep_ref, next_send_ref):
    size = next_keep_ref.shape[0]
    next_keep_ref[...] = keep_ref[0:size, :] + got_ref[0:size, :].astype(F32)
    next_send_ref[...] = (keep_ref[size:, :] + got_ref[size:, :].astype(F32)).astype(BF16)


def _finish_kernel(scale, counts, *refs):
    parts, out_ref = refs[:-1], refs[-1]
    rows = parts[0].shape[0]
    lanes = out_ref.shape[0] // rows
    at = 0
    for count in counts:
        total = parts[0][...]
        for more in parts[1:count]:
            total = total + more[...].astype(F32)
        parts = parts[count:]
        total = total * scale
        for j in range(0, total.shape[1], 128):
            out_ref[pl.ds(at, rows, stride=lanes), :] = total[:, j : j + 128]
            at += 1


def _after(value, *others):
    return lax.optimization_barrier((value,) + others)[0]


VM = pl.BlockSpec(memory_space=pltpu.VMEM)
SM = pl.BlockSpec(memory_space=pltpu.SMEM)


def _call(body, name, outs, in_specs, out_specs, mib, flops=0, scratch=(), **more):
    return pl.pallas_call(
        body,
        out_shape=outs,
        in_specs=in_specs,
        out_specs=out_specs,
        scratch_shapes=scratch,
        compiler_params=pltpu.CompilerParams(vmem_limit_bytes=mib * MIB),
        cost_estimate=pl.CostEstimate(flops=flops, bytes_accessed=4 * MIB, transcendentals=0),
        name=name,
        **more,
    )


def _shape(shape, dtype):
    return jax.ShapeDtypeStruct(shape, dtype)


def _fast(grad_tokens, routes, combine, down_weight, saved_pre):
    n_d, n_e = lax.axis_size("dp"), lax.axis_size("expert")
    tokens, width = grad_tokens.shape
    hidden = down_weight.shape[1]
    capacity = saved_pre.shape[3]
    rows = hidden // n_d
    depth = n_e * tokens
    lanes = width // 128
    where = jnp.stack([lax.axis_index("dp"), lax.axis_index("expert")]).astype(jnp.int32)
    pre = saved_pre.reshape(saved_pre.shape[1:])[0]
    sizes = [part * width // 16 for part in SIXTEENTHS]
    lead = sizes[0]

    whole = lambda i: (0, 0)
    first = _call(
        functools.partial(_pack_kernel, tokens, lead),
        "pack_tokens",
        _shape((tokens + INFO_ROWS, lead), BF16),
        [
            pl.BlockSpec((routes.shape[1], tokens), whole),
            pl.BlockSpec((routes.shape[1], tokens), whole),
            pl.BlockSpec((tokens, lead), whole),
        ],
        pl.BlockSpec((tokens + INFO_ROWS, lead), whole),
        PACK_MIB,
        grid=(1,),
    )(routes.T, combine.T, grad_tokens)
    rest = grad_tokens[:, lead:]

    def gather(block, *later):
        held = {0: block}
        for bit in reversed(range(n_e.bit_length() - 1)):
            for key in sorted(held):
                if later and bit == 0:
                    held[key] = _after(held[key], *later)
                held[key | (1 << bit)] = _send(held[key], 0, 1 << bit)
        return [held[j] for j in range(n_e)]

    firsts = gather(first, rest)

    act = _call(
        functools.partial(_activate_kernel, hidden),
        "activation",
        _shape((n_e, capacity, hidden), F32),
        [VM],
        VM,
        6,
    )(pre)

    last = tuple(range(2, n_d.bit_length() - 1))
    by_x, by_z, at_once = ((0,), (1,), last), ((1,), last, (0,)), ((0,), (1,) + last)

    def blocks_of(stages):
        blocks = [0]
        for b in [b for group in stages for b in group]:
            blocks = [q | (v << b) for q in blocks for v in (0, 1)]
        kept = len(blocks) >> len(stages[0])
        return tuple(blocks[:kept]), tuple(blocks[kept:])

    def halves(kept, sent, size):
        return _shape((kept * rows, size), F32), _shape((sent * rows, size), BF16)

    def exchange(send, size, group):
        got = []
        for v in range(1, 1 << len(group)):
            mask = sum((1 << b) for i, b in enumerate(group) if (v >> (len(group) - 1 - i)) & 1)
            got.append(_send(send[(v - 1) * size : v * size], mask, 0))
        return got

    def merge(keep, got):
        for more in got[:-1]:
            keep = keep + more.astype(F32)
        return keep, got[-1]

    def add(keep, got, group):
        keep, got = merge(keep, got)
        size = keep.shape[0] // rows
        kept = size >> len(group)
        return _call(
            _sum_kernel,
            "sum_halves",
            halves(kept, size - kept, keep.shape[1]),
            [VM, VM],
            (VM, VM),
            8,
        )(keep, got)

    kept, sent = blocks_of(by_x)
    at_all, keep_a, send_a = _call(
        functools.partial(_first_kernel, n_e, n_d, kept, sent),
        "first_partial",
        (_shape((hidden, depth), BF16),) + halves(len(kept), len(sent), lead),
        [SM] + [VM] * (1 + n_e),
        (VM, VM, VM),
        10,
        2 * hidden * depth * lead,
        [pltpu.VMEM((hidden, depth), BF16)],
    )(where, act, *firsts)
    got_a = exchange(send_a, keep_a.shape[0], by_x[0])

    raw_lead = _call(
        functools.partial(_lead_kernel, n_e, capacity),
        "raw_lead",
        _shape((n_e * capacity, hidden), F32),
        [SM] + [VM] * (1 + n_e),
        VM,
        10,
        LEAD_FLOPS,
        [pltpu.VMEM((n_e * capacity, lead), BF16)],
    )(_after(where, send_a), down_weight, *firsts)

    rests = gather(_after(rest, firsts[n_e // 2]), raw_lead)

    def partial(chunk, stages):
        kept, sent = blocks_of(stages)
        start = sum(sizes[1:chunk])
        columns = slice(start, start + sizes[chunk])
        return _call(
            functools.partial(_partial_kernel, n_e, kept, sent, rows, columns),
            "partial_chunk",
            halves(len(kept), len(sent), sizes[chunk]),
            [VM] * (1 + n_e),
            (VM, VM),
            8,
            2 * hidden * depth * sizes[chunk],
        )(at_all, *rests)

    keep_b, send_b = partial(1, by_x)
    keep_c, send_c = partial(2, at_once)
    keep_z, send_z = partial(3, by_z)

    got_z = exchange(send_z, keep_z.shape[0], by_z[0])
    pre_grad, back = _call(
        functools.partial(_slot_kernel, n_e, hidden),
        "slot_gradients",
        (_shape(pre.shape, BF16), _shape((n_e, 1, tokens), F32)),
        [SM] + [VM] * (3 + 2 * n_e),
        (VM, VM),
        14,
        2 * n_e * capacity * (width - lead) * hidden,
        [pltpu.VMEM((n_e * capacity, width - lead), BF16)],
    )(_after(where, send_b, send_c, send_z), pre, down_weight, raw_lead, *firsts, *rests)
    keep_z, send_z = add(keep_z, got_z, by_z[1])
    got_z = exchange(send_z, keep_z.shape[0], by_z[1])

    got_b = exchange(_after(send_b, back, send_z, *got_a), keep_b.shape[0], by_x[0])
    keep_a, send_a = add(_after(keep_a, back, send_z), got_a, by_x[1])
    got_a = exchange(send_a, keep_a.shape[0], by_x[1])

    returned = lax.all_to_all(
        _after(back, send_a, send_z), "expert", split_axis=0, concat_axis=0, tiled=True
    )

    got_c = exchange(_after(send_c, returned, *got_b, *got_z, *got_a), keep_c.shape[0], at_once[0])
    keep_b, send_b = add(keep_b, got_b, by_x[1])
    got_b = exchange(send_b, keep_b.shape[0], by_x[1])
    keep_a, send_a = add(keep_a, got_a, by_x[2])
    end_a = [keep_a] + exchange(send_a, keep_a.shape[0], by_x[2])
    keep_b, send_b = add(keep_b, got_b, by_x[2])
    end_b = [keep_b] + exchange(send_b, keep_b.shape[0], by_x[2])

    keep_c, send_c = add(_after(keep_c, send_b, end_a[1]), got_c, at_once[1])
    end_c = [keep_c] + exchange(send_c, keep_c.shape[0], at_once[1])
    keep_z, send_z = add(_after(keep_z, send_c), got_z, by_z[2])
    end_z = [keep_z] + exchange(send_z, keep_z.shape[0], by_z[2])
    ends = (end_a, end_b, end_c, end_z)
    down_grad = _call(
        functools.partial(_finish_kernel, 1.0 / n_d, tuple(len(end) for end in ends)),
        "finish",
        _shape((rows * lanes, 128), F32),
        [VM] * sum(len(end) for end in ends),
        VM,
        8,
    )(*[part for end in ends for part in end]).reshape(1, rows * width)

    gate_grad = sum(jnp.where(routes.T == k, returned[k], 0.0) for k in range(n_e)).T
    return pre_grad.reshape(saved_pre.shape), down_grad, gate_grad


def _general(grad_tokens, routes, combine, down_weight, saved_pre):
    experts = lax.axis_size("expert")
    tok_rows, route_count = routes.shape
    capacity = saved_pre.shape[3]
    model_width = grad_tokens.shape[1]
    hidden = down_weight.shape[1]
    flat_routes = routes.reshape(-1)
    onehot = (flat_routes[:, None] == jnp.arange(experts, dtype=jnp.int32)[None, :]).astype(jnp.int32)
    before = jnp.cumsum(onehot, axis=0) - onehot
    position = jnp.sum(before * onehot, axis=1)
    slot_id = flat_routes * capacity + position
    slot_grid = jnp.arange(experts * capacity, dtype=jnp.int32)
    chosen = slot_grid[:, None] == slot_id[None, :]
    placing = jnp.any(chosen.reshape(experts * capacity, tok_rows, route_count), axis=2).astype(BF16)
    outgoing = jnp.dot(placing, grad_tokens, preferred_element_type=F32).astype(BF16)
    combine_flat = combine.reshape(-1).astype(F32)
    out_weight = jnp.sum(jnp.where(chosen, combine_flat[None, :], 0.0), axis=1).astype(BF16)
    swap = functools.partial(lax.all_to_all, axis_name="expert", split_axis=0, concat_axis=0, tiled=True)
    slot_rows = swap(outgoing.reshape(experts, capacity, model_width)).reshape(-1, model_width)
    slot_weight = swap(out_weight.reshape(experts, capacity)).reshape(-1).astype(F32)
    raw_grad = lax.dot_general(
        slot_rows, down_weight[0], (((1,), (1,)), ((), ())), preferred_element_type=F32
    )
    pre_acts = saved_pre.reshape(-1, 2 * hidden).astype(F32)
    gate_pre, up_pre = pre_acts[:, :hidden], pre_acts[:, hidden:]
    logistic = jax.nn.sigmoid(gate_pre)
    activated = gate_pre * logistic
    hidden_act = activated * up_pre
    slot_gate = jnp.sum(hidden_act * raw_grad, axis=1)
    hidden_delta = slot_weight[:, None] * raw_grad
    gate_delta = hidden_delta * up_pre * logistic * (1.0 + gate_pre * (1.0 - logistic))
    pre_grad = jnp.concatenate([gate_delta, hidden_delta * activated], axis=1).astype(BF16)
    scaled = (slot_weight[:, None] * hidden_act).astype(BF16)
    whole_term = lax.dot_general(
        scaled, slot_rows, (((0,), (0,)), ((), ())), preferred_element_type=F32
    )
    summed = lax.psum_scatter(whole_term.reshape(-1), "dp", scatter_dimension=0, tiled=True)
    down_grad = (summed / lax.axis_size("dp"))[None]
    returned_flat = swap(slot_gate.reshape(experts, capacity)).reshape(-1)
    gate_flat = jnp.sum(jnp.where(chosen, returned_flat[:, None], 0.0), axis=0)
    return pre_grad.reshape(saved_pre.shape), down_grad, gate_flat.reshape(tok_rows, route_count)


def solution(mesh):
    n_d, n_e = mesh.shape["dp"], mesh.shape["expert"]

    def per_device(grad_tokens, routes, combine, down_weight, saved_pre):
        hidden, width = down_weight.shape[1:]
        whole_tiles = (
            hidden % (16 * n_d) == 0
            and saved_pre.shape[3] % 16 == 0
            and width % 2048 == 0
            and grad_tokens.shape[0] == 128
            and n_d >= 8
            and n_d & (n_d - 1) == 0
            and n_e >= 2
            and n_e & (n_e - 1) == 0
            and routes.shape[1] == 2
        )
        form = _fast if whole_tiles else _general
        return form(grad_tokens, routes, combine, down_weight, saved_pre)

    by_both = P(("dp", "expert"), None)
    by_expert = P("expert", "dp", None, None, None)
    return jax.shard_map(
        per_device,
        mesh=mesh,
        in_specs=(by_both, by_both, by_both, P("expert", None, None), by_expert),
        out_specs=(by_expert, P("expert", "dp"), by_both),
        check_vma=False,
    )
```

```python
import functools

import jax
import jax.numpy as jnp
from jax import lax
from jax.experimental import pallas as pl
from jax.experimental.pallas import tpu as pltpu
from jax.sharding import PartitionSpec as P

F32 = jnp.float32
BF16 = jnp.bfloat16
AXES = ("dp", "expert")
MIB = 1024 * 1024
INFO_ROWS = 16
PACK_MIB = 60
LEAD_FLOPS = 6 * 10**9
SIXTEENTHS = {"a": 5, "z": 4, "b": 4, "c": 3}


def _send(value, dp_mask, expert_mask):
    dps, experts = lax.axis_size("dp"), lax.axis_size("expert")
    pairs = [
        (d * experts + e, (d ^ dp_mask) * experts + (e ^ expert_mask))
        for d in range(dps)
        for e in range(experts)
    ]
    return lax.ppermute(value, AXES, pairs)


def _choice(info, expert, capacity):
    tokens = info.shape[1]
    first, second = info[0:1, :] == expert, info[1:2, :] == expert
    named = jnp.where(first | second, 1.0, 0.0)
    weight = jnp.where(first, info[2:3, :], 0.0) + jnp.where(second, info[3:4, :], 0.0)
    row = lax.broadcasted_iota(jnp.int32, (tokens, tokens), 0)
    col = lax.broadcasted_iota(jnp.int32, (tokens, tokens), 1)
    earlier = jnp.where(row < col, 1.0, 0.0).astype(BF16)
    position = jnp.dot(
        jnp.broadcast_to(named, (8, tokens)).astype(BF16), earlier, preferred_element_type=F32
    )[0:1, :]
    slot = lax.broadcasted_iota(jnp.int32, (capacity, tokens), 0).astype(F32)
    chosen = jnp.where((slot == position) & (named > 0.0), 1.0, 0.0)
    slot_weight = jnp.sum(chosen * weight, axis=1, keepdims=True)
    return chosen, slot_weight


def _pack_kernel(tokens, lead, routes_ref, combine_ref, tok_ref, first_ref):
    first_ref[0:tokens, :] = tok_ref[...]
    first_ref[tokens:, :] = jnp.zeros((INFO_ROWS, lead), BF16)
    info = jnp.concatenate(
        [
            routes_ref[...].astype(F32),
            combine_ref[...].astype(F32),
            jnp.zeros((INFO_ROWS - 4, tokens), F32),
        ],
        axis=0,
    )
    first_ref[tokens:, 0:tokens] = info.astype(BF16)


def _activate_kernel(hidden, pre_ref, out_ref):
    for j in range(pre_ref.shape[0]):
        pre = pre_ref[j].astype(F32)
        gate, up = pre[:, :hidden], pre[:, hidden:]
        out_ref[j] = gate * jax.nn.sigmoid(gate) * up


def _info(ref, tokens):
    return ref[tokens : tokens + INFO_ROWS, 0:tokens].astype(F32)


def _split(prod, keep_blocks, send_blocks, rows, keep_ref, send_ref):
    for p, q in enumerate(keep_blocks):
        keep_ref[p * rows : (p + 1) * rows, :] = prod[q * rows : (q + 1) * rows, :]
    for p, q in enumerate(send_blocks):
        send_ref[p * rows : (p + 1) * rows, :] = prod[q * rows : (q + 1) * rows, :].astype(BF16)


def _first_kernel(n_e, n_d, blocks_a, blocks_z, where_ref, act_ref, *refs):
    firsts, (at_ref, keep_a_ref, send_a_ref, keep_z_ref, send_z_ref, held) = refs[:n_e], refs[n_e:]
    d, e = where_ref[0], where_ref[1]
    expert = e.astype(F32)
    capacity, hidden = act_ref.shape[1:]
    tokens = firsts[0].shape[0] - INFO_ROWS
    rows = hidden // n_d
    for j in range(n_e):
        chosen, slot_weight = _choice(_info(firsts[j], tokens), expert, capacity)
        scaled = (slot_weight * act_ref[e ^ j]).astype(BF16)
        held[:, j * tokens : (j + 1) * tokens] = lax.dot_general(
            scaled, chosen.astype(BF16), (((0,), (0,)), ((), ())), preferred_element_type=F32
        ).astype(BF16)
    for q in range(n_d):
        start = pl.multiple_of((d ^ q) * rows, 16)
        at_ref[q * rows : (q + 1) * rows, :] = held[pl.ds(start, rows), :]
    tok = jnp.concatenate([r[0:tokens, :] for r in firsts], axis=0)
    prod = jnp.dot(at_ref[...], tok, preferred_element_type=F32)
    size = keep_a_ref.shape[1]
    _split(prod[:, :size], *blocks_a, rows, keep_a_ref, send_a_ref)
    _split(prod[:, size:], *blocks_z, rows, keep_z_ref, send_z_ref)


def _partial_kernel(n_e, keep_blocks, send_blocks, rows, columns, at_ref, *refs):
    tok = jnp.concatenate([r[:, columns] for r in refs[:n_e]], axis=0)
    prod = jnp.dot(at_ref[...], tok, preferred_element_type=F32)
    _split(prod, keep_blocks, send_blocks, rows, *refs[n_e:])


def _lead_kernel(n_e, capacity, where_ref, w_ref, *refs):
    firsts, raw_ref, rows_ref = refs[:n_e], refs[n_e], refs[n_e + 1]
    expert = where_ref[1].astype(F32)
    lead = firsts[0].shape[1]
    tokens = firsts[0].shape[0] - INFO_ROWS
    for j in range(n_e):
        chosen, _ = _choice(_info(firsts[j], tokens), expert, capacity)
        rows_ref[j * capacity : (j + 1) * capacity, :] = jnp.dot(
            chosen.astype(BF16), firsts[j][0:tokens, :], preferred_element_type=F32
        ).astype(BF16)
    raw_ref[...] = lax.dot_general(
        rows_ref[...], w_ref[0, :, 0:lead], (((1,), (1,)), ((), ())), preferred_element_type=F32
    )


def _slot_kernel(n_e, hidden, where_ref, pre_ref, w_ref, raw_ref, *refs):
    infos, rests, (pre_grad_ref, back_ref, rows_ref) = refs[:n_e], refs[n_e : 2 * n_e], refs[2 * n_e :]
    e = where_ref[1]
    expert = e.astype(F32)
    capacity = pre_ref.shape[1]
    tokens = rests[0].shape[0]
    lead = infos[0].shape[1]
    picks, weights = [], []
    for j in range(n_e):
        chosen, slot_weight = _choice(_info(infos[j], tokens), expert, capacity)
        picks.append(chosen)
        weights.append(slot_weight)
        rows_ref[j * capacity : (j + 1) * capacity, :] = jnp.dot(
            chosen.astype(BF16), rests[j][...], preferred_element_type=F32
        ).astype(BF16)
    tile = 256 if hidden % 256 == 0 else hidden
    gates = [jnp.zeros((capacity, 1), F32) for _ in range(n_e)]
    for h in range(0, hidden, tile):
        raw_all = raw_ref[:, h : h + tile] + lax.dot_general(
            rows_ref[...],
            w_ref[0, h : h + tile, lead:],
            (((1,), (1,)), ((), ())),
            preferred_element_type=F32,
        )
        for j in range(n_e):
            raw = raw_all[j * capacity : (j + 1) * capacity, :]
            a = pre_ref[e ^ j, :, h : h + tile].astype(F32)
            u = pre_ref[e ^ j, :, hidden + h : hidden + h + tile].astype(F32)
            s = jax.nn.sigmoid(a)
            silu = a * s
            gates[j] = gates[j] + jnp.sum(silu * u * raw, axis=1, keepdims=True)
            delta = weights[j] * raw
            pre_grad_ref[e ^ j, :, h : h + tile] = (delta * u * s * (1.0 + a * (1.0 - s))).astype(BF16)
            pre_grad_ref[e ^ j, :, hidden + h : hidden + h + tile] = (delta * silu).astype(BF16)
    for j in range(n_e):
        back_ref[e ^ j] = jnp.sum(picks[j] * gates[j], axis=0, keepdims=True)


def _sum_kernel(keep_ref, got_ref, next_keep_ref, next_send_ref):
    size = next_keep_ref.shape[0]
    next_keep_ref[...] = keep_ref[0:size, :] + got_ref[0:size, :].astype(F32)
    next_send_ref[...] = (keep_ref[size:, :] + got_ref[size:, :].astype(F32)).astype(BF16)


def _finish_kernel(scale, counts, *refs):
    parts, out_ref = refs[:-1], refs[-1]
    rows = parts[0].shape[0]
    lanes = out_ref.shape[0] // rows
    at = 0
    for count in counts:
        total = parts[0][...]
        for more in parts[1:count]:
            total = total + more[...].astype(F32)
        parts = parts[count:]
        total = total * scale
        for j in range(0, total.shape[1], 128):
            out_ref[pl.ds(at, rows, stride=lanes), :] = total[:, j : j + 128]
            at += 1


def _after(value, *others):
    return lax.optimization_barrier((value,) + others)[0]


VM = pl.BlockSpec(memory_space=pltpu.VMEM)
SM = pl.BlockSpec(memory_space=pltpu.SMEM)


def _call(body, name, outs, in_specs, out_specs, mib, flops=0, scratch=(), **more):
    return pl.pallas_call(
        body,
        out_shape=outs,
        in_specs=in_specs,
        out_specs=out_specs,
        scratch_shapes=scratch,
        compiler_params=pltpu.CompilerParams(vmem_limit_bytes=mib * MIB),
        cost_estimate=pl.CostEstimate(flops=flops, bytes_accessed=0, transcendentals=0),
        name=name,
        **more,
    )


def _shape(shape, dtype):
    return jax.ShapeDtypeStruct(shape, dtype)


def _fast(grad_tokens, routes, combine, down_weight, saved_pre):
    n_d, n_e = lax.axis_size("dp"), lax.axis_size("expert")
    tokens, width = grad_tokens.shape
    hidden = down_weight.shape[1]
    capacity = saved_pre.shape[3]
    rows = hidden // n_d
    depth = n_e * tokens
    lanes = width // 128
    where = jnp.stack([lax.axis_index("dp"), lax.axis_index("expert")]).astype(jnp.int32)
    pre = saved_pre.reshape(saved_pre.shape[1:])[0]
    sizes = {name: part * width // 16 for name, part in SIXTEENTHS.items()}
    lead = sizes["a"] + sizes["z"]

    whole = lambda i: (0, 0)
    first = _call(
        functools.partial(_pack_kernel, tokens, lead),
        "pack_tokens",
        _shape((tokens + INFO_ROWS, lead), BF16),
        [
            pl.BlockSpec((routes.shape[1], tokens), whole),
            pl.BlockSpec((routes.shape[1], tokens), whole),
            pl.BlockSpec((tokens, lead), whole),
        ],
        pl.BlockSpec((tokens + INFO_ROWS, lead), whole),
        PACK_MIB,
        grid=(1,),
    )(routes.T, combine.T, grad_tokens)
    rest = grad_tokens[:, lead:]

    def gather(block, *later):
        held = {0: block}
        for bit in reversed(range(n_e.bit_length() - 1)):
            for key in sorted(held):
                if later and bit == 0:
                    held[key] = _after(held[key], *later)
                held[key | (1 << bit)] = _send(held[key], 0, 1 << bit)
        return [held[j] for j in range(n_e)]

    firsts = gather(first, rest)

    act = _call(
        functools.partial(_activate_kernel, hidden),
        "activation",
        _shape((n_e, capacity, hidden), F32),
        [VM],
        VM,
        6,
    )(pre)

    last = tuple(range(2, n_d.bit_length() - 1))
    by_x, by_z, at_once = ((0,), (1,), last), ((1,), last, (0,)), ((0,), (1,) + last)

    def blocks_of(stages):
        blocks = [0]
        for b in [b for group in stages for b in group]:
            blocks = [q | (v << b) for q in blocks for v in (0, 1)]
        kept = len(blocks) >> len(stages[0])
        return tuple(blocks[:kept]), tuple(blocks[kept:])

    def halves(kept, sent, size):
        return _shape((kept * rows, size), F32), _shape((sent * rows, size), BF16)

    def exchange(send, size, group):
        got = []
        for v in range(1, 1 << len(group)):
            mask = sum((1 << b) for i, b in enumerate(group) if (v >> (len(group) - 1 - i)) & 1)
            got.append(_send(send[(v - 1) * size : v * size], mask, 0))
        return got

    def merge(keep, got):
        for more in got[:-1]:
            keep = keep + more.astype(F32)
        return keep, got[-1]

    def add(keep, got, group):
        keep, got = merge(keep, got)
        size = keep.shape[0] // rows
        kept = size >> len(group)
        return _call(
            _sum_kernel,
            "sum_halves",
            halves(kept, size - kept, keep.shape[1]),
            [VM, VM],
            (VM, VM),
            8,
        )(keep, got)

    blocks_a, blocks_z = blocks_of(by_x), blocks_of(by_z)
    at_all, keep_a, send_a, keep_z, send_z = _call(
        functools.partial(_first_kernel, n_e, n_d, blocks_a, blocks_z),
        "first_partial",
        (_shape((hidden, depth), BF16),)
        + halves(*map(len, blocks_a), sizes["a"])
        + halves(*map(len, blocks_z), sizes["z"]),
        [SM] + [VM] * (1 + n_e),
        (VM,) * 5,
        14,
        2 * hidden * depth * lead,
        [pltpu.VMEM((hidden, depth), BF16)],
    )(where, act, *firsts)
    got_a = exchange(send_a, keep_a.shape[0], by_x[0])
    got_z = exchange(send_z, keep_z.shape[0], by_z[0])

    raw_lead = _call(
        functools.partial(_lead_kernel, n_e, capacity),
        "raw_lead",
        _shape((n_e * capacity, hidden), F32),
        [SM] + [VM] * (1 + n_e),
        VM,
        10,
        LEAD_FLOPS,
        [pltpu.VMEM((n_e * capacity, lead), BF16)],
    )(_after(where, send_a), down_weight, *firsts)

    rests = gather(_after(rest, firsts[n_e // 2]), raw_lead)

    def partial(start, size, stages):
        kept, sent = blocks_of(stages)
        return _call(
            functools.partial(_partial_kernel, n_e, kept, sent, rows, slice(start, start + size)),
            "partial_chunk",
            halves(len(kept), len(sent), size),
            [VM] * (1 + n_e),
            (VM, VM),
            8,
            0,
        )(at_all, *rests)

    keep_b, send_b = partial(0, sizes["b"], by_x)
    keep_c, send_c = partial(sizes["b"], sizes["c"], at_once)

    pre_grad, back = _call(
        functools.partial(_slot_kernel, n_e, hidden),
        "slot_gradients",
        (_shape(pre.shape, BF16), _shape((n_e, 1, tokens), F32)),
        [SM] + [VM] * (3 + 2 * n_e),
        (VM, VM),
        14,
        0,
        [pltpu.VMEM((n_e * capacity, width - lead), BF16)],
    )(_after(where, send_b, send_c), pre, down_weight, raw_lead, *firsts, *rests)
    got_b = exchange(_after(send_b, back, *got_a), keep_b.shape[0], by_x[0])
    keep_a, send_a = add(_after(keep_a, back), got_a, by_x[1])
    got_a = exchange(send_a, keep_a.shape[0], by_x[1])
    keep_z, send_z = add(_after(keep_z, back), got_z, by_z[1])
    got_z = exchange(send_z, keep_z.shape[0], by_z[1])
    returned = lax.all_to_all(
        _after(back, send_a, send_z), "expert", split_axis=0, concat_axis=0, tiled=True
    )

    got_c = exchange(_after(send_c, returned, *got_b, *got_z, *got_a), keep_c.shape[0], at_once[0])
    keep_b, send_b = add(keep_b, got_b, by_x[1])
    got_b = exchange(send_b, keep_b.shape[0], by_x[1])
    keep_a, send_a = add(_after(keep_a, send_b), got_a, by_x[2])
    end_a = [keep_a] + exchange(send_a, keep_a.shape[0], by_x[2])
    keep_z, send_z = add(_after(keep_z, send_a, send_b), got_z, by_z[2])
    end_z = [keep_z] + exchange(send_z, keep_z.shape[0], by_z[2])
    keep_b, send_b = add(keep_b, got_b, by_x[2])
    end_b = [keep_b] + exchange(send_b, keep_b.shape[0], by_x[2])

    keep_c, send_c = add(_after(keep_c, send_b, end_a[1], end_z[1]), got_c, at_once[1])
    end_c = [keep_c] + exchange(send_c, keep_c.shape[0], at_once[1])

    ends = (end_a, end_z, end_b, end_c)
    down_grad = _call(
        functools.partial(_finish_kernel, 1.0 / n_d, tuple(len(end) for end in ends)),
        "finish",
        _shape((rows * lanes, 128), F32),
        [VM] * sum(len(end) for end in ends),
        VM,
        8,
    )(*[part for end in ends for part in end]).reshape(1, rows * width)

    gate_grad = sum(jnp.where(routes.T == k, returned[k], 0.0) for k in range(n_e)).T
    return pre_grad.reshape(saved_pre.shape), down_grad, gate_grad


def _general(grad_tokens, routes, combine, down_weight, saved_pre):
    experts = lax.axis_size("expert")
    tok_rows, route_count = routes.shape
    capacity = saved_pre.shape[3]
    model_width = grad_tokens.shape[1]
    hidden = down_weight.shape[1]
    flat_routes = routes.reshape(-1)
    onehot = (flat_routes[:, None] == jnp.arange(experts, dtype=jnp.int32)[None, :]).astype(jnp.int32)
    before = jnp.cumsum(onehot, axis=0) - onehot
    position = jnp.sum(before * onehot, axis=1)
    slot_id = flat_routes * capacity + position
    slot_grid = jnp.arange(experts * capacity, dtype=jnp.int32)
    chosen = slot_grid[:, None] == slot_id[None, :]
    placing = jnp.any(chosen.reshape(experts * capacity, tok_rows, route_count), axis=2).astype(BF16)
    outgoing = jnp.dot(placing, grad_tokens, preferred_element_type=F32).astype(BF16)
    combine_flat = combine.reshape(-1).astype(F32)
    out_weight = jnp.sum(jnp.where(chosen, combine_flat[None, :], 0.0), axis=1).astype(BF16)
    swap = functools.partial(lax.all_to_all, axis_name="expert", split_axis=0, concat_axis=0, tiled=True)
    slot_rows = swap(outgoing.reshape(experts, capacity, model_width)).reshape(-1, model_width)
    slot_weight = swap(out_weight.reshape(experts, capacity)).reshape(-1).astype(F32)
    raw_grad = lax.dot_general(
        slot_rows, down_weight[0], (((1,), (1,)), ((), ())), preferred_element_type=F32
    )
    pre_acts = saved_pre.reshape(-1, 2 * hidden).astype(F32)
    gate_pre, up_pre = pre_acts[:, :hidden], pre_acts[:, hidden:]
    logistic = jax.nn.sigmoid(gate_pre)
    activated = gate_pre * logistic
    hidden_act = activated * up_pre
    slot_gate = jnp.sum(hidden_act * raw_grad, axis=1)
    hidden_delta = slot_weight[:, None] * raw_grad
    gate_delta = hidden_delta * up_pre * logistic * (1.0 + gate_pre * (1.0 - logistic))
    pre_grad = jnp.concatenate([gate_delta, hidden_delta * activated], axis=1).astype(BF16)
    scaled = (slot_weight[:, None] * hidden_act).astype(BF16)
    whole_term = lax.dot_general(
        scaled, slot_rows, (((0,), (0,)), ((), ())), preferred_element_type=F32
    )
    summed = lax.psum_scatter(whole_term.reshape(-1), "dp", scatter_dimension=0, tiled=True)
    down_grad = (summed / lax.axis_size("dp"))[None]
    returned_flat = swap(slot_gate.reshape(experts, capacity)).reshape(-1)
    gate_flat = jnp.sum(jnp.where(chosen, returned_flat[:, None], 0.0), axis=0)
    return pre_grad.reshape(saved_pre.shape), down_grad, gate_flat.reshape(tok_rows, route_count)


def solution(mesh):
    n_d, n_e = mesh.shape["dp"], mesh.shape["expert"]

    def per_device(grad_tokens, routes, combine, down_weight, saved_pre):
        hidden, width = down_weight.shape[1:]
        whole_tiles = (
            hidden % (16 * n_d) == 0
            and saved_pre.shape[3] % 16 == 0
            and width % 2048 == 0
            and grad_tokens.shape[0] == 128
            and n_d >= 8
            and n_d & (n_d - 1) == 0
            and n_e >= 2
            and n_e & (n_e - 1) == 0
            and routes.shape[1] == 2
        )
        form = _fast if whole_tiles else _general
        return form(grad_tokens, routes, combine, down_weight, saved_pre)

    by_both = P(("dp", "expert"), None)
    by_expert = P("expert", "dp", None, None, None)
    return jax.shard_map(
        per_device,
        mesh=mesh,
        in_specs=(by_both, by_both, by_both, P("expert", None, None), by_expert),
        out_specs=(by_expert, P("expert", "dp"), by_both),
        check_vma=False,
    )
```

```python
import functools

import jax
import jax.numpy as jnp
from jax import lax
from jax.experimental import pallas as pl
from jax.experimental.pallas import tpu as pltpu
from jax.sharding import PartitionSpec as P

F32 = jnp.float32
BF16 = jnp.bfloat16
AXES = ("dp", "expert")
MIB = 1024 * 1024
INFO_ROWS = 16
PACK_MIB = 8
LEAD_FLOPS = 6 * 10**9
SIXTEENTHS = {"a": 5, "z": 4, "b": 4, "c": 3}


def _send(value, dp_mask, expert_mask):
    dps, experts = lax.axis_size("dp"), lax.axis_size("expert")
    pairs = [
        (d * experts + e, (d ^ dp_mask) * experts + (e ^ expert_mask))
        for d in range(dps)
        for e in range(experts)
    ]
    return lax.ppermute(value, AXES, pairs)


def _choice(info, expert, capacity):
    tokens = info.shape[1]
    first, second = info[0:1, :] == expert, info[1:2, :] == expert
    named = jnp.where(first | second, 1.0, 0.0)
    weight = jnp.where(first, info[2:3, :], 0.0) + jnp.where(second, info[3:4, :], 0.0)
    row = lax.broadcasted_iota(jnp.int32, (tokens, tokens), 0)
    col = lax.broadcasted_iota(jnp.int32, (tokens, tokens), 1)
    earlier = jnp.where(row < col, 1.0, 0.0).astype(BF16)
    position = jnp.dot(
        jnp.broadcast_to(named, (8, tokens)).astype(BF16), earlier, preferred_element_type=F32
    )[0:1, :]
    slot = lax.broadcasted_iota(jnp.int32, (capacity, tokens), 0).astype(F32)
    chosen = jnp.where((slot == position) & (named > 0.0), 1.0, 0.0)
    slot_weight = jnp.sum(chosen * weight, axis=1, keepdims=True)
    return chosen, slot_weight


def _pack_kernel(tokens, lead, routes_ref, combine_ref, tok_ref, first_ref):
    first_ref[0:tokens, :] = tok_ref[...]
    first_ref[tokens:, :] = jnp.zeros((INFO_ROWS, lead), BF16)
    info = jnp.concatenate(
        [
            routes_ref[...].astype(F32),
            combine_ref[...].astype(F32),
            jnp.zeros((INFO_ROWS - 4, tokens), F32),
        ],
        axis=0,
    )
    first_ref[tokens:, 0:tokens] = info.astype(BF16)


def _activate_kernel(hidden, pre_ref, out_ref):
    for j in range(pre_ref.shape[0]):
        pre = pre_ref[j].astype(F32)
        gate, up = pre[:, :hidden], pre[:, hidden:]
        out_ref[j] = gate * jax.nn.sigmoid(gate) * up


def _info(ref, tokens):
    return ref[tokens : tokens + INFO_ROWS, 0:tokens].astype(F32)


def _split(prod, keep_blocks, send_blocks, rows, keep_ref, send_ref):
    for p, q in enumerate(keep_blocks):
        keep_ref[p * rows : (p + 1) * rows, :] = prod[q * rows : (q + 1) * rows, :]
    for p, q in enumerate(send_blocks):
        send_ref[p * rows : (p + 1) * rows, :] = prod[q * rows : (q + 1) * rows, :].astype(BF16)


def _first_kernel(n_e, n_d, blocks_a, blocks_z, where_ref, act_ref, *refs):
    firsts, (at_ref, keep_a_ref, send_a_ref, keep_z_ref, send_z_ref, held) = refs[:n_e], refs[n_e:]
    d, e = where_ref[0], where_ref[1]
    expert = e.astype(F32)
    capacity, hidden = act_ref.shape[1:]
    tokens = firsts[0].shape[0] - INFO_ROWS
    rows = hidden // n_d
    for j in range(n_e):
        chosen, slot_weight = _choice(_info(firsts[j], tokens), expert, capacity)
        scaled = (slot_weight * act_ref[e ^ j]).astype(BF16)
        held[:, j * tokens : (j + 1) * tokens] = lax.dot_general(
            scaled, chosen.astype(BF16), (((0,), (0,)), ((), ())), preferred_element_type=F32
        ).astype(BF16)
    for q in range(n_d):
        start = pl.multiple_of((d ^ q) * rows, 16)
        at_ref[q * rows : (q + 1) * rows, :] = held[pl.ds(start, rows), :]
    tok = jnp.concatenate([r[0:tokens, :] for r in firsts], axis=0)
    prod = jnp.dot(at_ref[...], tok, preferred_element_type=F32)
    size = keep_a_ref.shape[1]
    _split(prod[:, :size], *blocks_a, rows, keep_a_ref, send_a_ref)
    _split(prod[:, size:], *blocks_z, rows, keep_z_ref, send_z_ref)


def _partial_kernel(n_e, keep_blocks, send_blocks, rows, columns, at_ref, *refs):
    tok = jnp.concatenate([r[:, columns] for r in refs[:n_e]], axis=0)
    prod = jnp.dot(at_ref[...], tok, preferred_element_type=F32)
    _split(prod, keep_blocks, send_blocks, rows, *refs[n_e:])


def _lead_kernel(n_e, capacity, where_ref, w_ref, *refs):
    firsts, raw_ref, rows_ref = refs[:n_e], refs[n_e], refs[n_e + 1]
    expert = where_ref[1].astype(F32)
    lead = firsts[0].shape[1]
    tokens = firsts[0].shape[0] - INFO_ROWS
    for j in range(n_e):
        chosen, _ = _choice(_info(firsts[j], tokens), expert, capacity)
        rows_ref[j * capacity : (j + 1) * capacity, :] = jnp.dot(
            chosen.astype(BF16), firsts[j][0:tokens, :], preferred_element_type=F32
        ).astype(BF16)
    raw_ref[...] = lax.dot_general(
        rows_ref[...], w_ref[0, :, 0:lead], (((1,), (1,)), ((), ())), preferred_element_type=F32
    )


def _slot_kernel(n_e, hidden, where_ref, pre_ref, w_ref, raw_ref, *refs):
    infos, rests, (pre_grad_ref, back_ref, rows_ref) = refs[:n_e], refs[n_e : 2 * n_e], refs[2 * n_e :]
    e = where_ref[1]
    expert = e.astype(F32)
    capacity = pre_ref.shape[1]
    tokens = rests[0].shape[0]
    lead = infos[0].shape[1]
    picks, weights = [], []
    for j in range(n_e):
        chosen, slot_weight = _choice(_info(infos[j], tokens), expert, capacity)
        picks.append(chosen)
        weights.append(slot_weight)
        rows_ref[j * capacity : (j + 1) * capacity, :] = jnp.dot(
            chosen.astype(BF16), rests[j][...], preferred_element_type=F32
        ).astype(BF16)
    tile = 256 if hidden % 256 == 0 else hidden
    gates = [jnp.zeros((capacity, 1), F32) for _ in range(n_e)]
    for h in range(0, hidden, tile):
        raw_all = raw_ref[:, h : h + tile] + lax.dot_general(
            rows_ref[...],
            w_ref[0, h : h + tile, lead:],
            (((1,), (1,)), ((), ())),
            preferred_element_type=F32,
        )
        for j in range(n_e):
            raw = raw_all[j * capacity : (j + 1) * capacity, :]
            a = pre_ref[e ^ j, :, h : h + tile].astype(F32)
            u = pre_ref[e ^ j, :, hidden + h : hidden + h + tile].astype(F32)
            s = jax.nn.sigmoid(a)
            silu = a * s
            gates[j] = gates[j] + jnp.sum(silu * u * raw, axis=1, keepdims=True)
            delta = weights[j] * raw
            pre_grad_ref[e ^ j, :, h : h + tile] = (delta * u * s * (1.0 + a * (1.0 - s))).astype(BF16)
            pre_grad_ref[e ^ j, :, hidden + h : hidden + h + tile] = (delta * silu).astype(BF16)
    for j in range(n_e):
        back_ref[e ^ j] = jnp.sum(picks[j] * gates[j], axis=0, keepdims=True)


def _sum_kernel(keep_ref, got_ref, next_keep_ref, next_send_ref):
    size = next_keep_ref.shape[0]
    next_keep_ref[...] = keep_ref[0:size, :] + got_ref[0:size, :].astype(F32)
    next_send_ref[...] = (keep_ref[size:, :] + got_ref[size:, :].astype(F32)).astype(BF16)


def _finish_kernel(scale, counts, *refs):
    parts, out_ref = refs[:-1], refs[-1]
    rows = parts[0].shape[0]
    lanes = out_ref.shape[0] // rows
    at = 0
    for count in counts:
        total = parts[0][...]
        for more in parts[1:count]:
            total = total + more[...].astype(F32)
        parts = parts[count:]
        total = total * scale
        for j in range(0, total.shape[1], 128):
            out_ref[pl.ds(at, rows, stride=lanes), :] = total[:, j : j + 128]
            at += 1


def _after(value, *others):
    return lax.optimization_barrier((value,) + others)[0]


VM = pl.BlockSpec(memory_space=pltpu.VMEM)
SM = pl.BlockSpec(memory_space=pltpu.SMEM)


def _call(body, name, outs, in_specs, out_specs, mib, flops=0, scratch=(), **more):
    return pl.pallas_call(
        body,
        out_shape=outs,
        in_specs=in_specs,
        out_specs=out_specs,
        scratch_shapes=scratch,
        compiler_params=pltpu.CompilerParams(vmem_limit_bytes=mib * MIB),
        cost_estimate=pl.CostEstimate(flops=flops, bytes_accessed=0, transcendentals=0),
        name=name,
        **more,
    )


def _shape(shape, dtype):
    return jax.ShapeDtypeStruct(shape, dtype)


def _fast(grad_tokens, routes, combine, down_weight, saved_pre):
    n_d, n_e = lax.axis_size("dp"), lax.axis_size("expert")
    tokens, width = grad_tokens.shape
    hidden = down_weight.shape[1]
    capacity = saved_pre.shape[3]
    rows = hidden // n_d
    depth = n_e * tokens
    lanes = width // 128
    where = jnp.stack([lax.axis_index("dp"), lax.axis_index("expert")]).astype(jnp.int32)
    pre = saved_pre.reshape(saved_pre.shape[1:])[0]
    sizes = {name: part * width // 16 for name, part in SIXTEENTHS.items()}
    lead = sizes["a"] + sizes["z"]

    whole = lambda i: (0, 0)
    first = _call(
        functools.partial(_pack_kernel, tokens, lead),
        "pack_tokens",
        pltpu.VMEM((tokens + INFO_ROWS, lead), BF16),
        [
            pl.BlockSpec((routes.shape[1], tokens), whole),
            pl.BlockSpec((routes.shape[1], tokens), whole),
            pl.BlockSpec((tokens, lead), whole),
        ],
        VM,
        PACK_MIB,
        grid=(1,),
    )(*(pltpu.with_memory_space_constraint(v, pltpu.HBM) for v in (routes.T, combine.T, grad_tokens)))
    rest = grad_tokens[:, lead:]

    def gather(block, *later):
        held = {0: block}
        for bit in reversed(range(n_e.bit_length() - 1)):
            for key in sorted(held):
                if later and bit == 0:
                    held[key] = _after(held[key], *later)
                held[key | (1 << bit)] = _send(held[key], 0, 1 << bit)
        return [held[j] for j in range(n_e)]

    firsts = gather(first, rest)

    act = _call(
        functools.partial(_activate_kernel, hidden),
        "activation",
        _shape((n_e, capacity, hidden), F32),
        [VM],
        VM,
        6,
    )(pre)

    last = tuple(range(2, n_d.bit_length() - 1))
    by_x, by_z, at_once = ((0,), (1,), last), ((1,), last, (0,)), ((0,), (1,) + last)

    def blocks_of(stages):
        blocks = [0]
        for b in [b for group in stages for b in group]:
            blocks = [q | (v << b) for q in blocks for v in (0, 1)]
        kept = len(blocks) >> len(stages[0])
        return tuple(blocks[:kept]), tuple(blocks[kept:])

    def halves(kept, sent, size):
        return _shape((kept * rows, size), F32), _shape((sent * rows, size), BF16)

    def exchange(send, size, group):
        got = []
        for v in range(1, 1 << len(group)):
            mask = sum((1 << b) for i, b in enumerate(group) if (v >> (len(group) - 1 - i)) & 1)
            got.append(_send(send[(v - 1) * size : v * size], mask, 0))
        return got

    def merge(keep, got):
        for more in got[:-1]:
            keep = keep + more.astype(F32)
        return keep, got[-1]

    def add(keep, got, group):
        keep, got = merge(keep, got)
        size = keep.shape[0] // rows
        kept = size >> len(group)
        return _call(
            _sum_kernel,
            "sum_halves",
            halves(kept, size - kept, keep.shape[1]),
            [VM, VM],
            (VM, VM),
            8,
        )(keep, got)

    blocks_a, blocks_z = blocks_of(by_x), blocks_of(by_z)
    at_all, keep_a, send_a, keep_z, send_z = _call(
        functools.partial(_first_kernel, n_e, n_d, blocks_a, blocks_z),
        "first_partial",
        (_shape((hidden, depth), BF16),)
        + halves(*map(len, blocks_a), sizes["a"])
        + halves(*map(len, blocks_z), sizes["z"]),
        [SM] + [VM] * (1 + n_e),
        (VM,) * 5,
        14,
        2 * hidden * depth * lead,
        [pltpu.VMEM((hidden, depth), BF16)],
    )(where, act, *firsts)
    got_a = exchange(send_a, keep_a.shape[0], by_x[0])
    got_z = exchange(send_z, keep_z.shape[0], by_z[0])

    raw_lead = _call(
        functools.partial(_lead_kernel, n_e, capacity),
        "raw_lead",
        _shape((n_e * capacity, hidden), F32),
        [SM] + [VM] * (1 + n_e),
        VM,
        10,
        LEAD_FLOPS,
        [pltpu.VMEM((n_e * capacity, lead), BF16)],
    )(_after(where, send_a), down_weight, *firsts)

    rests = gather(_after(rest, firsts[n_e // 2]), raw_lead)

    def partial(start, size, stages):
        kept, sent = blocks_of(stages)
        return _call(
            functools.partial(_partial_kernel, n_e, kept, sent, rows, slice(start, start + size)),
            "partial_chunk",
            halves(len(kept), len(sent), size),
            [VM] * (1 + n_e),
            (VM, VM),
            8,
            0,
        )(at_all, *rests)

    keep_b, send_b = partial(0, sizes["b"], by_x)
    keep_c, send_c = partial(sizes["b"], sizes["c"], at_once)

    pre_grad, back = _call(
        functools.partial(_slot_kernel, n_e, hidden),
        "slot_gradients",
        (_shape(pre.shape, BF16), _shape((n_e, 1, tokens), F32)),
        [SM] + [VM] * (3 + 2 * n_e),
        (VM, VM),
        14,
        0,
        [pltpu.VMEM((n_e * capacity, width - lead), BF16)],
    )(_after(where, send_b, send_c), pre, down_weight, raw_lead, *firsts, *rests)
    keep_z, send_z = add(_after(keep_z, back), got_z, by_z[1])
    got_z = exchange(send_z, keep_z.shape[0], by_z[1])
    got_b = exchange(_after(send_b, back, send_z, *got_a), keep_b.shape[0], by_x[0])
    keep_a, send_a = add(_after(keep_a, back), got_a, by_x[1])
    got_a = exchange(send_a, keep_a.shape[0], by_x[1])
    returned = lax.all_to_all(
        _after(back, send_a, send_z), "expert", split_axis=0, concat_axis=0, tiled=True
    )

    got_c = exchange(_after(send_c, returned, *got_b), keep_c.shape[0], at_once[0])
    keep_b, send_b = add(keep_b, got_b, by_x[1])
    got_b = exchange(send_b, keep_b.shape[0], by_x[1])
    keep_a, send_a = add(_after(keep_a, send_b), got_a, by_x[2])
    end_a = [keep_a] + exchange(send_a, keep_a.shape[0], by_x[2])
    keep_z, send_z = add(_after(keep_z, send_a, send_b), got_z, by_z[2])
    end_z = [keep_z] + exchange(send_z, keep_z.shape[0], by_z[2])
    keep_b, send_b = add(keep_b, got_b, by_x[2])
    end_b = [keep_b] + exchange(send_b, keep_b.shape[0], by_x[2])

    keep_c, send_c = add(_after(keep_c, send_b, end_a[1], end_z[1]), got_c, at_once[1])
    end_c = [keep_c] + exchange(send_c, keep_c.shape[0], at_once[1])

    ends = (end_a, end_z, end_b, end_c)
    down_grad = _call(
        functools.partial(_finish_kernel, 1.0 / n_d, tuple(len(end) for end in ends)),
        "finish",
        _shape((rows * lanes, 128), F32),
        [VM] * sum(len(end) for end in ends),
        VM,
        8,
    )(*[part for end in ends for part in end]).reshape(1, rows * width)

    gate_grad = sum(jnp.where(routes.T == k, returned[k], 0.0) for k in range(n_e)).T
    return pre_grad.reshape(saved_pre.shape), down_grad, gate_grad


def _general(grad_tokens, routes, combine, down_weight, saved_pre):
    experts = lax.axis_size("expert")
    tok_rows, route_count = routes.shape
    capacity = saved_pre.shape[3]
    model_width = grad_tokens.shape[1]
    hidden = down_weight.shape[1]
    flat_routes = routes.reshape(-1)
    onehot = (flat_routes[:, None] == jnp.arange(experts, dtype=jnp.int32)[None, :]).astype(jnp.int32)
    before = jnp.cumsum(onehot, axis=0) - onehot
    position = jnp.sum(before * onehot, axis=1)
    slot_id = flat_routes * capacity + position
    slot_grid = jnp.arange(experts * capacity, dtype=jnp.int32)
    chosen = slot_grid[:, None] == slot_id[None, :]
    placing = jnp.any(chosen.reshape(experts * capacity, tok_rows, route_count), axis=2).astype(BF16)
    outgoing = jnp.dot(placing, grad_tokens, preferred_element_type=F32).astype(BF16)
    combine_flat = combine.reshape(-1).astype(F32)
    out_weight = jnp.sum(jnp.where(chosen, combine_flat[None, :], 0.0), axis=1).astype(BF16)
    swap = functools.partial(lax.all_to_all, axis_name="expert", split_axis=0, concat_axis=0, tiled=True)
    slot_rows = swap(outgoing.reshape(experts, capacity, model_width)).reshape(-1, model_width)
    slot_weight = swap(out_weight.reshape(experts, capacity)).reshape(-1).astype(F32)
    raw_grad = lax.dot_general(
        slot_rows, down_weight[0], (((1,), (1,)), ((), ())), preferred_element_type=F32
    )
    pre_acts = saved_pre.reshape(-1, 2 * hidden).astype(F32)
    gate_pre, up_pre = pre_acts[:, :hidden], pre_acts[:, hidden:]
    logistic = jax.nn.sigmoid(gate_pre)
    activated = gate_pre * logistic
    hidden_act = activated * up_pre
    slot_gate = jnp.sum(hidden_act * raw_grad, axis=1)
    hidden_delta = slot_weight[:, None] * raw_grad
    gate_delta = hidden_delta * up_pre * logistic * (1.0 + gate_pre * (1.0 - logistic))
    pre_grad = jnp.concatenate([gate_delta, hidden_delta * activated], axis=1).astype(BF16)
    scaled = (slot_weight[:, None] * hidden_act).astype(BF16)
    whole_term = lax.dot_general(
        scaled, slot_rows, (((0,), (0,)), ((), ())), preferred_element_type=F32
    )
    summed = lax.psum_scatter(whole_term.reshape(-1), "dp", scatter_dimension=0, tiled=True)
    down_grad = (summed / lax.axis_size("dp"))[None]
    returned_flat = swap(slot_gate.reshape(experts, capacity)).reshape(-1)
    gate_flat = jnp.sum(jnp.where(chosen, returned_flat[:, None], 0.0), axis=0)
    return pre_grad.reshape(saved_pre.shape), down_grad, gate_flat.reshape(tok_rows, route_count)


def solution(mesh):
    n_d, n_e = mesh.shape["dp"], mesh.shape["expert"]

    def per_device(grad_tokens, routes, combine, down_weight, saved_pre):
        hidden, width = down_weight.shape[1:]
        whole_tiles = (
            hidden % (16 * n_d) == 0
            and saved_pre.shape[3] % 16 == 0
            and width % 2048 == 0
            and grad_tokens.shape[0] == 128
            and n_d >= 8
            and n_d & (n_d - 1) == 0
            and n_e >= 2
            and n_e & (n_e - 1) == 0
            and routes.shape[1] == 2
        )
        form = _fast if whole_tiles else _general
        return form(grad_tokens, routes, combine, down_weight, saved_pre)

    by_both = P(("dp", "expert"), None)
    by_expert = P("expert", "dp", None, None, None)
    return jax.shard_map(
        per_device,
        mesh=mesh,
        in_specs=(by_both, by_both, by_both, P("expert", None, None), by_expert),
        out_specs=(by_expert, P("expert", "dp"), by_both),
        check_vma=False,
    )
```

```python
import functools

import jax
import jax.numpy as jnp
from jax import lax
from jax.experimental import pallas as pl
from jax.experimental.pallas import tpu as pltpu
from jax.sharding import PartitionSpec as P

F32 = jnp.float32
BF16 = jnp.bfloat16
AXES = ("dp", "expert")
MIB = 1024 * 1024
INFO_ROWS = 16
PACK_MIB = 8
LEAD_FLOPS = 6 * 10**9
SIXTEENTHS = {"a": 5, "z": 4, "b": 4, "c": 3}


def _send(value, dp_mask, expert_mask):
    dps, experts = lax.axis_size("dp"), lax.axis_size("expert")
    pairs = [
        (d * experts + e, (d ^ dp_mask) * experts + (e ^ expert_mask))
        for d in range(dps)
        for e in range(experts)
    ]
    return lax.ppermute(value, AXES, pairs)


def _choice(info, expert, capacity):
    tokens = info.shape[1]
    first, second = info[0:1, :] == expert, info[1:2, :] == expert
    named = jnp.where(first | second, 1.0, 0.0)
    weight = jnp.where(first, info[2:3, :], 0.0) + jnp.where(second, info[3:4, :], 0.0)
    row = lax.broadcasted_iota(jnp.int32, (tokens, tokens), 0)
    col = lax.broadcasted_iota(jnp.int32, (tokens, tokens), 1)
    earlier = jnp.where(row < col, 1.0, 0.0).astype(BF16)
    position = jnp.dot(
        jnp.broadcast_to(named, (8, tokens)).astype(BF16), earlier, preferred_element_type=F32
    )[0:1, :]
    slot = lax.broadcasted_iota(jnp.int32, (capacity, tokens), 0).astype(F32)
    chosen = jnp.where((slot == position) & (named > 0.0), 1.0, 0.0)
    slot_weight = jnp.sum(chosen * weight, axis=1, keepdims=True)
    return chosen, slot_weight


def _pack_kernel(tokens, lead, routes_ref, combine_ref, tok_ref, first_ref):
    first_ref[0:tokens, :] = tok_ref[...]
    first_ref[tokens:, :] = jnp.zeros((INFO_ROWS, lead), BF16)
    info = jnp.concatenate(
        [
            routes_ref[...].astype(F32),
            combine_ref[...].astype(F32),
            jnp.zeros((INFO_ROWS - 4, tokens), F32),
        ],
        axis=0,
    )
    first_ref[tokens:, 0:tokens] = info.astype(BF16)


def _activate_kernel(hidden, pre_ref, out_ref):
    for j in range(pre_ref.shape[0]):
        pre = pre_ref[j].astype(F32)
        gate, up = pre[:, :hidden], pre[:, hidden:]
        out_ref[j] = gate * jax.nn.sigmoid(gate) * up


def _info(ref, tokens):
    return ref[tokens : tokens + INFO_ROWS, 0:tokens].astype(F32)


def _split(prod, keep_blocks, send_blocks, rows, keep_ref, send_ref):
    for p, q in enumerate(keep_blocks):
        keep_ref[p * rows : (p + 1) * rows, :] = prod[q * rows : (q + 1) * rows, :]
    for p, q in enumerate(send_blocks):
        send_ref[p * rows : (p + 1) * rows, :] = prod[q * rows : (q + 1) * rows, :].astype(BF16)


def _some_rows(at_ref, blocks, rows):
    return jnp.concatenate([at_ref[q * rows : (q + 1) * rows, :] for q in blocks], axis=0)


def _first_kernel(n_e, n_d, sent, where_ref, act_ref, *refs):
    firsts, (at_ref, send_ref, held) = refs[:n_e], refs[n_e:]
    d, e = where_ref[0], where_ref[1]
    expert = e.astype(F32)
    capacity, hidden = act_ref.shape[1:]
    tokens = firsts[0].shape[0] - INFO_ROWS
    rows = hidden // n_d
    none = jnp.zeros((capacity, tokens), F32)
    for j in range(0, n_e, 2):
        left, left_weight = _choice(_info(firsts[j], tokens), expert, capacity)
        right, right_weight = _choice(_info(firsts[j + 1], tokens), expert, capacity)
        scaled = jnp.concatenate(
            [left_weight * act_ref[e ^ j], right_weight * act_ref[e ^ (j + 1)]], axis=0
        ).astype(BF16)
        chosen = jnp.concatenate(
            [
                jnp.concatenate([left, none], axis=1),
                jnp.concatenate([none, right], axis=1),
            ],
            axis=0,
        ).astype(BF16)
        held[:, j * tokens : (j + 2) * tokens] = lax.dot_general(
            scaled, chosen, (((0,), (0,)), ((), ())), preferred_element_type=F32
        ).astype(BF16)
    for q in range(n_d):
        start = pl.multiple_of((d ^ q) * rows, 16)
        at_ref[q * rows : (q + 1) * rows, :] = held[pl.ds(start, rows), :]
    tok = jnp.concatenate([r[0:tokens, : send_ref.shape[1]] for r in firsts], axis=0)
    send_ref[...] = jnp.dot(
        _some_rows(at_ref, sent, rows), tok, preferred_element_type=F32
    ).astype(BF16)


def _second_kernel(n_e, kept, blocks_z, rows, at_ref, *refs):
    firsts, (keep_a_ref, keep_z_ref, send_z_ref) = refs[:n_e], refs[n_e:]
    tokens = firsts[0].shape[0] - INFO_ROWS
    size = keep_a_ref.shape[1]
    tok = jnp.concatenate([r[0:tokens, size:] for r in firsts], axis=0)
    prod = jnp.dot(at_ref[...], tok, preferred_element_type=F32)
    _split(prod, *blocks_z, rows, keep_z_ref, send_z_ref)
    tok = jnp.concatenate([r[0:tokens, :size] for r in firsts], axis=0)
    keep_a_ref[...] = jnp.dot(_some_rows(at_ref, kept, rows), tok, preferred_element_type=F32)


def _partial_kernel(n_e, keep_blocks, send_blocks, rows, columns, at_ref, *refs):
    tok = jnp.concatenate([r[:, columns] for r in refs[:n_e]], axis=0)
    prod = jnp.dot(at_ref[...], tok, preferred_element_type=F32)
    _split(prod, keep_blocks, send_blocks, rows, *refs[n_e:])


def _lead_kernel(n_e, capacity, where_ref, w_ref, *refs):
    firsts, raw_ref, rows_ref = refs[:n_e], refs[n_e], refs[n_e + 1]
    expert = where_ref[1].astype(F32)
    lead = firsts[0].shape[1]
    tokens = firsts[0].shape[0] - INFO_ROWS
    for j in range(n_e):
        chosen, _ = _choice(_info(firsts[j], tokens), expert, capacity)
        rows_ref[j * capacity : (j + 1) * capacity, :] = jnp.dot(
            chosen.astype(BF16), firsts[j][0:tokens, :], preferred_element_type=F32
        ).astype(BF16)
    raw_ref[...] = lax.dot_general(
        rows_ref[...], w_ref[0, :, 0:lead], (((1,), (1,)), ((), ())), preferred_element_type=F32
    )


def _slot_kernel(n_e, hidden, where_ref, pre_ref, w_ref, raw_ref, *refs):
    infos, rests, (pre_grad_ref, back_ref, rows_ref) = refs[:n_e], refs[n_e : 2 * n_e], refs[2 * n_e :]
    e = where_ref[1]
    expert = e.astype(F32)
    capacity = pre_ref.shape[1]
    tokens = rests[0].shape[0]
    lead = infos[0].shape[1]
    picks, weights = [], []
    for j in range(n_e):
        chosen, slot_weight = _choice(_info(infos[j], tokens), expert, capacity)
        picks.append(chosen)
        weights.append(slot_weight)
        rows_ref[j * capacity : (j + 1) * capacity, :] = jnp.dot(
            chosen.astype(BF16), rests[j][...], preferred_element_type=F32
        ).astype(BF16)
    tile = 256 if hidden % 256 == 0 else hidden
    gates = [jnp.zeros((capacity, 1), F32) for _ in range(n_e)]
    for h in range(0, hidden, tile):
        raw_all = raw_ref[:, h : h + tile] + lax.dot_general(
            rows_ref[...],
            w_ref[0, h : h + tile, lead:],
            (((1,), (1,)), ((), ())),
            preferred_element_type=F32,
        )
        for j in range(n_e):
            raw = raw_all[j * capacity : (j + 1) * capacity, :]
            a = pre_ref[e ^ j, :, h : h + tile].astype(F32)
            u = pre_ref[e ^ j, :, hidden + h : hidden + h + tile].astype(F32)
            s = jax.nn.sigmoid(a)
            silu = a * s
            gates[j] = gates[j] + jnp.sum(silu * u * raw, axis=1, keepdims=True)
            delta = weights[j] * raw
            pre_grad_ref[e ^ j, :, h : h + tile] = (delta * u * s * (1.0 + a * (1.0 - s))).astype(BF16)
            pre_grad_ref[e ^ j, :, hidden + h : hidden + h + tile] = (delta * silu).astype(BF16)
    for j in range(n_e):
        back_ref[e ^ j] = jnp.sum(picks[j] * gates[j], axis=0, keepdims=True)


def _sum_kernel(keep_ref, got_ref, next_keep_ref, next_send_ref):
    size = next_keep_ref.shape[0]
    next_keep_ref[...] = keep_ref[0:size, :] + got_ref[0:size, :].astype(F32)
    next_send_ref[...] = (keep_ref[size:, :] + got_ref[size:, :].astype(F32)).astype(BF16)


def _finish_kernel(scale, counts, *refs):
    parts, out_ref = refs[:-1], refs[-1]
    rows = parts[0].shape[0]
    lanes = out_ref.shape[0] // rows
    at = 0
    for count in counts:
        total = parts[0][...]
        for more in parts[1:count]:
            total = total + more[...].astype(F32)
        parts = parts[count:]
        total = total * scale
        for j in range(0, total.shape[1], 128):
            out_ref[pl.ds(at, rows, stride=lanes), :] = total[:, j : j + 128]
            at += 1


def _after(value, *others):
    return lax.optimization_barrier((value,) + others)[0]


VM = pl.BlockSpec(memory_space=pltpu.VMEM)
SM = pl.BlockSpec(memory_space=pltpu.SMEM)


def _call(body, name, outs, in_specs, out_specs, mib, flops=0, scratch=(), **more):
    return pl.pallas_call(
        body,
        out_shape=outs,
        in_specs=in_specs,
        out_specs=out_specs,
        scratch_shapes=scratch,
        compiler_params=pltpu.CompilerParams(vmem_limit_bytes=mib * MIB),
        cost_estimate=pl.CostEstimate(flops=flops, bytes_accessed=0, transcendentals=0),
        name=name,
        **more,
    )


def _shape(shape, dtype):
    return jax.ShapeDtypeStruct(shape, dtype)


def _fast(grad_tokens, routes, combine, down_weight, saved_pre):
    n_d, n_e = lax.axis_size("dp"), lax.axis_size("expert")
    tokens, width = grad_tokens.shape
    hidden = down_weight.shape[1]
    capacity = saved_pre.shape[3]
    rows = hidden // n_d
    depth = n_e * tokens
    lanes = width // 128
    where = jnp.stack([lax.axis_index("dp"), lax.axis_index("expert")]).astype(jnp.int32)
    pre = saved_pre.reshape(saved_pre.shape[1:])[0]
    sizes = {name: part * width // 16 for name, part in SIXTEENTHS.items()}
    lead = sizes["a"] + sizes["z"]

    whole = lambda i: (0, 0)
    first = _call(
        functools.partial(_pack_kernel, tokens, lead),
        "pack_tokens",
        pltpu.VMEM((tokens + INFO_ROWS, lead), BF16),
        [
            pl.BlockSpec((routes.shape[1], tokens), whole),
            pl.BlockSpec((routes.shape[1], tokens), whole),
            pl.BlockSpec((tokens, lead), whole),
        ],
        VM,
        PACK_MIB,
        grid=(1,),
    )(*(pltpu.with_memory_space_constraint(v, pltpu.HBM) for v in (routes.T, combine.T, grad_tokens)))
    rest = grad_tokens[:, lead:]

    def gather(block, *later):
        held = {0: block}
        for bit in reversed(range(n_e.bit_length() - 1)):
            for key in sorted(held):
                if later and bit == 0:
                    held[key] = _after(held[key], *later)
                held[key | (1 << bit)] = _send(held[key], 0, 1 << bit)
        return [held[j] for j in range(n_e)]

    firsts = gather(first, rest)

    act = _call(
        functools.partial(_activate_kernel, hidden),
        "activation",
        _shape((n_e, capacity, hidden), F32),
        [VM],
        VM,
        6,
    )(pre)

    last = tuple(range(2, n_d.bit_length() - 1))
    by_x, by_z, at_once = ((0,), (1,), last), ((1,), last, (0,)), ((0,), (1,) + last)

    def blocks_of(stages):
        blocks = [0]
        for b in [b for group in stages for b in group]:
            blocks = [q | (v << b) for q in blocks for v in (0, 1)]
        kept = len(blocks) >> len(stages[0])
        return tuple(blocks[:kept]), tuple(blocks[kept:])

    def halves(kept, sent, size):
        return _shape((kept * rows, size), F32), _shape((sent * rows, size), BF16)

    def exchange(send, size, group):
        got = []
        for v in range(1, 1 << len(group)):
            mask = sum((1 << b) for i, b in enumerate(group) if (v >> (len(group) - 1 - i)) & 1)
            got.append(_send(send[(v - 1) * size : v * size], mask, 0))
        return got

    def merge(keep, got):
        for more in got[:-1]:
            keep = keep + more.astype(F32)
        return keep, got[-1]

    def add(keep, got, group):
        keep, got = merge(keep, got)
        size = keep.shape[0] // rows
        kept = size >> len(group)
        return _call(
            _sum_kernel,
            "sum_halves",
            halves(kept, size - kept, keep.shape[1]),
            [VM, VM],
            (VM, VM),
            8,
        )(keep, got)

    blocks_a, blocks_z = blocks_of(by_x), blocks_of(by_z)
    keep_shape, send_shape = halves(*map(len, blocks_a), sizes["a"])
    at_all, send_a = _call(
        functools.partial(_first_kernel, n_e, n_d, blocks_a[1]),
        "first_send",
        (_shape((hidden, depth), BF16), send_shape),
        [SM] + [VM] * (1 + n_e),
        (VM, VM),
        12,
        0,
        [pltpu.VMEM((hidden, depth), BF16)],
    )(where, act, *firsts)
    keep_a, keep_z, send_z = _call(
        functools.partial(_second_kernel, n_e, blocks_a[0], blocks_z, rows),
        "first_keep",
        (keep_shape,) + halves(*map(len, blocks_z), sizes["z"]),
        [VM] * (1 + n_e),
        (VM,) * 3,
        12,
    )(_after(at_all, send_a), *firsts)
    got_a = exchange(send_a, keep_a.shape[0], by_x[0])
    got_z = exchange(send_z, keep_z.shape[0], by_z[0])

    raw_lead = _call(
        functools.partial(_lead_kernel, n_e, capacity),
        "raw_lead",
        _shape((n_e * capacity, hidden), F32),
        [SM] + [VM] * (1 + n_e),
        VM,
        10,
        LEAD_FLOPS,
        [pltpu.VMEM((n_e * capacity, lead), BF16)],
    )(_after(where, send_a), down_weight, *firsts)

    rests = gather(_after(rest, firsts[n_e // 2]), raw_lead)

    def partial(start, size, stages):
        kept, sent = blocks_of(stages)
        return _call(
            functools.partial(_partial_kernel, n_e, kept, sent, rows, slice(start, start + size)),
            "partial_chunk",
            halves(len(kept), len(sent), size),
            [VM] * (1 + n_e),
            (VM, VM),
            8,
            0,
        )(at_all, *rests)

    keep_b, send_b = partial(0, sizes["b"], by_x)
    keep_c, send_c = partial(sizes["b"], sizes["c"], at_once)

    pre_grad, back = _call(
        functools.partial(_slot_kernel, n_e, hidden),
        "slot_gradients",
        (_shape(pre.shape, BF16), _shape((n_e, 1, tokens), F32)),
        [SM] + [VM] * (3 + 2 * n_e),
        (VM, VM),
        14,
        0,
        [pltpu.VMEM((n_e * capacity, width - lead), BF16)],
    )(_after(where, send_b, send_c), pre, down_weight, raw_lead, *firsts, *rests)
    keep_z, send_z = add(_after(keep_z, back), got_z, by_z[1])
    got_z = exchange(send_z, keep_z.shape[0], by_z[1])
    got_b = exchange(_after(send_b, back, send_z, *got_a), keep_b.shape[0], by_x[0])
    keep_a, send_a = add(_after(keep_a, back), got_a, by_x[1])
    got_a = exchange(send_a, keep_a.shape[0], by_x[1])
    returned = lax.all_to_all(
        _after(back, send_a, send_z), "expert", split_axis=0, concat_axis=0, tiled=True
    )

    got_c = exchange(_after(send_c, returned, *got_b), keep_c.shape[0], at_once[0])
    keep_b, send_b = add(keep_b, got_b, by_x[1])
    got_b = exchange(send_b, keep_b.shape[0], by_x[1])
    keep_a, send_a = add(_after(keep_a, send_b), got_a, by_x[2])
    end_a = [keep_a] + exchange(send_a, keep_a.shape[0], by_x[2])
    keep_z, send_z = add(_after(keep_z, send_a, send_b), got_z, by_z[2])
    end_z = [keep_z] + exchange(send_z, keep_z.shape[0], by_z[2])
    keep_b, send_b = add(keep_b, got_b, by_x[2])
    end_b = [keep_b] + exchange(send_b, keep_b.shape[0], by_x[2])

    keep_c, send_c = add(_after(keep_c, send_b, end_a[1], end_z[1]), got_c, at_once[1])
    end_c = [keep_c] + exchange(send_c, keep_c.shape[0], at_once[1])

    ends = (end_a, end_z, end_b, end_c)
    down_grad = _call(
        functools.partial(_finish_kernel, 1.0 / n_d, tuple(len(end) for end in ends)),
        "finish",
        _shape((rows * lanes, 128), F32),
        [VM] * sum(len(end) for end in ends),
        VM,
        8,
    )(*[part for end in ends for part in end]).reshape(1, rows * width)

    gate_grad = sum(jnp.where(routes.T == k, returned[k], 0.0) for k in range(n_e)).T
    return pre_grad.reshape(saved_pre.shape), down_grad, gate_grad


def _general(grad_tokens, routes, combine, down_weight, saved_pre):
    experts = lax.axis_size("expert")
    tok_rows, route_count = routes.shape
    capacity = saved_pre.shape[3]
    model_width = grad_tokens.shape[1]
    hidden = down_weight.shape[1]
    flat_routes = routes.reshape(-1)
    onehot = (flat_routes[:, None] == jnp.arange(experts, dtype=jnp.int32)[None, :]).astype(jnp.int32)
    before = jnp.cumsum(onehot, axis=0) - onehot
    position = jnp.sum(before * onehot, axis=1)
    slot_id = flat_routes * capacity + position
    slot_grid = jnp.arange(experts * capacity, dtype=jnp.int32)
    chosen = slot_grid[:, None] == slot_id[None, :]
    placing = jnp.any(chosen.reshape(experts * capacity, tok_rows, route_count), axis=2).astype(BF16)
    outgoing = jnp.dot(placing, grad_tokens, preferred_element_type=F32).astype(BF16)
    combine_flat = combine.reshape(-1).astype(F32)
    out_weight = jnp.sum(jnp.where(chosen, combine_flat[None, :], 0.0), axis=1).astype(BF16)
    swap = functools.partial(lax.all_to_all, axis_name="expert", split_axis=0, concat_axis=0, tiled=True)
    slot_rows = swap(outgoing.reshape(experts, capacity, model_width)).reshape(-1, model_width)
    slot_weight = swap(out_weight.reshape(experts, capacity)).reshape(-1).astype(F32)
    raw_grad = lax.dot_general(
        slot_rows, down_weight[0], (((1,), (1,)), ((), ())), preferred_element_type=F32
    )
    pre_acts = saved_pre.reshape(-1, 2 * hidden).astype(F32)
    gate_pre, up_pre = pre_acts[:, :hidden], pre_acts[:, hidden:]
    logistic = jax.nn.sigmoid(gate_pre)
    activated = gate_pre * logistic
    hidden_act = activated * up_pre
    slot_gate = jnp.sum(hidden_act * raw_grad, axis=1)
    hidden_delta = slot_weight[:, None] * raw_grad
    gate_delta = hidden_delta * up_pre * logistic * (1.0 + gate_pre * (1.0 - logistic))
    pre_grad = jnp.concatenate([gate_delta, hidden_delta * activated], axis=1).astype(BF16)
    scaled = (slot_weight[:, None] * hidden_act).astype(BF16)
    whole_term = lax.dot_general(
        scaled, slot_rows, (((0,), (0,)), ((), ())), preferred_element_type=F32
    )
    summed = lax.psum_scatter(whole_term.reshape(-1), "dp", scatter_dimension=0, tiled=True)
    down_grad = (summed / lax.axis_size("dp"))[None]
    returned_flat = swap(slot_gate.reshape(experts, capacity)).reshape(-1)
    gate_flat = jnp.sum(jnp.where(chosen, returned_flat[:, None], 0.0), axis=0)
    return pre_grad.reshape(saved_pre.shape), down_grad, gate_flat.reshape(tok_rows, route_count)


def solution(mesh):
    n_d, n_e = mesh.shape["dp"], mesh.shape["expert"]

    def per_device(grad_tokens, routes, combine, down_weight, saved_pre):
        hidden, width = down_weight.shape[1:]
        whole_tiles = (
            hidden % (16 * n_d) == 0
            and saved_pre.shape[3] % 16 == 0
            and width % 2048 == 0
            and grad_tokens.shape[0] == 128
            and n_d >= 8
            and n_d & (n_d - 1) == 0
            and n_e >= 2
            and n_e & (n_e - 1) == 0
            and routes.shape[1] == 2
        )
        form = _fast if whole_tiles else _general
        return form(grad_tokens, routes, combine, down_weight, saved_pre)

    by_both = P(("dp", "expert"), None)
    by_expert = P("expert", "dp", None, None, None)
    return jax.shard_map(
        per_device,
        mesh=mesh,
        in_specs=(by_both, by_both, by_both, P("expert", None, None), by_expert),
        out_specs=(by_expert, P("expert", "dp"), by_both),
        check_vma=False,
    )
```

```python
import functools

import jax
import jax.numpy as jnp
from jax import lax
from jax.experimental import pallas as pl
from jax.experimental.pallas import tpu as pltpu
from jax.sharding import PartitionSpec as P

F32 = jnp.float32
BF16 = jnp.bfloat16
AXES = ("dp", "expert")
MIB = 1024 * 1024
INFO_ROWS = 16
PACK_MIB = 8
LEAD_FLOPS = 6 * 10**9
SIXTEENTHS = {"a": 5, "z": 4, "b": 4, "c": 3}


def _send(value, dp_mask, expert_mask):
    dps, experts = lax.axis_size("dp"), lax.axis_size("expert")
    pairs = [
        (d * experts + e, (d ^ dp_mask) * experts + (e ^ expert_mask))
        for d in range(dps)
        for e in range(experts)
    ]
    return lax.ppermute(value, AXES, pairs)


def _choice(info, expert, capacity):
    tokens = info.shape[1]
    first, second = info[0:1, :] == expert, info[1:2, :] == expert
    named = jnp.where(first | second, 1.0, 0.0)
    weight = jnp.where(first, info[2:3, :], 0.0) + jnp.where(second, info[3:4, :], 0.0)
    row = lax.broadcasted_iota(jnp.int32, (tokens, tokens), 0)
    col = lax.broadcasted_iota(jnp.int32, (tokens, tokens), 1)
    earlier = jnp.where(row < col, 1.0, 0.0).astype(BF16)
    position = jnp.dot(
        jnp.broadcast_to(named, (8, tokens)).astype(BF16), earlier, preferred_element_type=F32
    )[0:1, :]
    slot = lax.broadcasted_iota(jnp.int32, (capacity, tokens), 0).astype(F32)
    chosen = jnp.where((slot == position) & (named > 0.0), 1.0, 0.0)
    slot_weight = jnp.sum(chosen * weight, axis=1, keepdims=True)
    return chosen, slot_weight


def _pack_kernel(tokens, lead, routes_ref, combine_ref, tok_ref, first_ref):
    first_ref[0:tokens, :] = tok_ref[...]
    first_ref[tokens:, :] = jnp.zeros((INFO_ROWS, lead), BF16)
    info = jnp.concatenate(
        [
            routes_ref[...].astype(F32),
            combine_ref[...].astype(F32),
            jnp.zeros((INFO_ROWS - 4, tokens), F32),
        ],
        axis=0,
    )
    first_ref[tokens:, 0:tokens] = info.astype(BF16)


def _activate_kernel(hidden, pre_ref, out_ref):
    for j in range(pre_ref.shape[0]):
        pre = pre_ref[j].astype(F32)
        gate, up = pre[:, :hidden], pre[:, hidden:]
        out_ref[j] = gate * jax.nn.sigmoid(gate) * up


def _info(ref, tokens):
    return ref[tokens : tokens + INFO_ROWS, 0:tokens].astype(F32)


def _split(prod, keep_blocks, send_blocks, rows, keep_ref, send_ref):
    for p, q in enumerate(keep_blocks):
        keep_ref[p * rows : (p + 1) * rows, :] = prod[q * rows : (q + 1) * rows, :]
    for p, q in enumerate(send_blocks):
        send_ref[p * rows : (p + 1) * rows, :] = prod[q * rows : (q + 1) * rows, :].astype(BF16)


def _some_rows(at_ref, blocks, rows):
    return jnp.concatenate([at_ref[q * rows : (q + 1) * rows, :] for q in blocks], axis=0)


def _first_kernel(n_e, n_d, sent, where_ref, act_ref, *refs):
    firsts, (at_ref, send_ref, held) = refs[:n_e], refs[n_e:]
    d, e = where_ref[0], where_ref[1]
    expert = e.astype(F32)
    capacity, hidden = act_ref.shape[1:]
    tokens = firsts[0].shape[0] - INFO_ROWS
    rows = hidden // n_d
    none = jnp.zeros((capacity, tokens), F32)
    for j in range(0, n_e, 2):
        left, left_weight = _choice(_info(firsts[j], tokens), expert, capacity)
        right, right_weight = _choice(_info(firsts[j + 1], tokens), expert, capacity)
        scaled = jnp.concatenate(
            [left_weight * act_ref[e ^ j], right_weight * act_ref[e ^ (j + 1)]], axis=0
        ).astype(BF16)
        chosen = jnp.concatenate(
            [
                jnp.concatenate([left, none], axis=1),
                jnp.concatenate([none, right], axis=1),
            ],
            axis=0,
        ).astype(BF16)
        held[:, j * tokens : (j + 2) * tokens] = lax.dot_general(
            scaled, chosen, (((0,), (0,)), ((), ())), preferred_element_type=F32
        ).astype(BF16)
    for q in range(n_d):
        start = pl.multiple_of((d ^ q) * rows, 16)
        at_ref[q * rows : (q + 1) * rows, :] = held[pl.ds(start, rows), :]
    tok = jnp.concatenate([r[0:tokens, : send_ref.shape[1]] for r in firsts], axis=0)
    send_ref[...] = jnp.dot(
        _some_rows(at_ref, sent, rows), tok, preferred_element_type=F32
    ).astype(BF16)


def _second_kernel(n_e, kept, blocks_z, rows, at_ref, *refs):
    firsts, (keep_a_ref, keep_z_ref, send_z_ref) = refs[:n_e], refs[n_e:]
    tokens = firsts[0].shape[0] - INFO_ROWS
    size = keep_a_ref.shape[1]
    tok = jnp.concatenate([r[0:tokens, size:] for r in firsts], axis=0)
    prod = jnp.dot(at_ref[...], tok, preferred_element_type=F32)
    _split(prod, *blocks_z, rows, keep_z_ref, send_z_ref)
    tok = jnp.concatenate([r[0:tokens, :size] for r in firsts], axis=0)
    keep_a_ref[...] = jnp.dot(_some_rows(at_ref, kept, rows), tok, preferred_element_type=F32)


def _partial_kernel(n_e, keep_blocks, send_blocks, rows, columns, at_ref, *refs):
    tok = jnp.concatenate([r[:, columns] for r in refs[:n_e]], axis=0)
    prod = jnp.dot(at_ref[...], tok, preferred_element_type=F32)
    _split(prod, keep_blocks, send_blocks, rows, *refs[n_e:])


def _lead_kernel(n_e, capacity, where_ref, w_ref, *refs):
    firsts, raw_ref, rows_ref = refs[:n_e], refs[n_e], refs[n_e + 1]
    expert = where_ref[1].astype(F32)
    lead = firsts[0].shape[1]
    tokens = firsts[0].shape[0] - INFO_ROWS
    for j in range(n_e):
        chosen, _ = _choice(_info(firsts[j], tokens), expert, capacity)
        rows_ref[j * capacity : (j + 1) * capacity, :] = jnp.dot(
            chosen.astype(BF16), firsts[j][0:tokens, :], preferred_element_type=F32
        ).astype(BF16)
    raw_ref[...] = lax.dot_general(
        rows_ref[...], w_ref[0, :, 0:lead], (((1,), (1,)), ((), ())), preferred_element_type=F32
    )


def _slot_kernel(n_e, hidden, where_ref, pre_ref, w_ref, raw_ref, *refs):
    infos, rests, (pre_grad_ref, back_ref, rows_ref) = refs[:n_e], refs[n_e : 2 * n_e], refs[2 * n_e :]
    e = where_ref[1]
    expert = e.astype(F32)
    capacity = pre_ref.shape[1]
    tokens = rests[0].shape[0]
    lead = infos[0].shape[1]
    picks, weights = [], []
    for j in range(n_e):
        chosen, slot_weight = _choice(_info(infos[j], tokens), expert, capacity)
        picks.append(chosen)
        weights.append(slot_weight)
        rows_ref[j * capacity : (j + 1) * capacity, :] = jnp.dot(
            chosen.astype(BF16), rests[j][...], preferred_element_type=F32
        ).astype(BF16)
    tile = 256 if hidden % 256 == 0 else hidden
    gates = [jnp.zeros((capacity, 1), F32) for _ in range(n_e)]
    for h in range(0, hidden, tile):
        raw_all = raw_ref[:, h : h + tile] + lax.dot_general(
            rows_ref[...],
            w_ref[0, h : h + tile, lead:],
            (((1,), (1,)), ((), ())),
            preferred_element_type=F32,
        )
        for j in range(n_e):
            raw = raw_all[j * capacity : (j + 1) * capacity, :]
            a = pre_ref[e ^ j, :, h : h + tile].astype(F32)
            u = pre_ref[e ^ j, :, hidden + h : hidden + h + tile].astype(F32)
            s = jax.nn.sigmoid(a)
            silu = a * s
            gates[j] = gates[j] + jnp.sum(silu * u * raw, axis=1, keepdims=True)
            delta = weights[j] * raw
            pre_grad_ref[e ^ j, :, h : h + tile] = (delta * u * s * (1.0 + a * (1.0 - s))).astype(BF16)
            pre_grad_ref[e ^ j, :, hidden + h : hidden + h + tile] = (delta * silu).astype(BF16)
    for j in range(n_e):
        back_ref[e ^ j] = jnp.sum(picks[j] * gates[j], axis=0, keepdims=True)


def _sum_kernel(keep_ref, got_ref, next_keep_ref, next_send_ref):
    size = next_keep_ref.shape[0]
    next_keep_ref[...] = keep_ref[0:size, :] + got_ref[0:size, :].astype(F32)
    next_send_ref[...] = (keep_ref[size:, :] + got_ref[size:, :].astype(F32)).astype(BF16)


def _finish_kernel(scale, first_lane, counts, *refs):
    parts, out_ref = refs[:-1], refs[-1]
    rows = parts[-1].shape[0]
    lanes = out_ref.shape[0] // rows
    if first_lane:
        out_ref[...] = parts[0][...]
        parts = parts[1:]
    at = first_lane
    for count in counts:
        total = parts[0][...]
        for more in parts[1:count]:
            total = total + more[...].astype(F32)
        parts = parts[count:]
        total = total * scale
        for j in range(0, total.shape[1], 128):
            out_ref[pl.ds(at, rows, stride=lanes), :] = total[:, j : j + 128]
            at += 1
    if not first_lane:
        for at in range(at, lanes):
            out_ref[pl.ds(at, rows, stride=lanes), :] = jnp.zeros((rows, 128), F32)


def _after(value, *others):
    return lax.optimization_barrier((value,) + others)[0]


VM = pl.BlockSpec(memory_space=pltpu.VMEM)
SM = pl.BlockSpec(memory_space=pltpu.SMEM)


def _call(body, name, outs, in_specs, out_specs, mib, flops=0, scratch=(), **more):
    return pl.pallas_call(
        body,
        out_shape=outs,
        in_specs=in_specs,
        out_specs=out_specs,
        scratch_shapes=scratch,
        compiler_params=pltpu.CompilerParams(vmem_limit_bytes=mib * MIB),
        cost_estimate=pl.CostEstimate(flops=flops, bytes_accessed=0, transcendentals=0),
        name=name,
        **more,
    )


def _shape(shape, dtype):
    return jax.ShapeDtypeStruct(shape, dtype)


def _fast(grad_tokens, routes, combine, down_weight, saved_pre):
    n_d, n_e = lax.axis_size("dp"), lax.axis_size("expert")
    tokens, width = grad_tokens.shape
    hidden = down_weight.shape[1]
    capacity = saved_pre.shape[3]
    rows = hidden // n_d
    depth = n_e * tokens
    lanes = width // 128
    where = jnp.stack([lax.axis_index("dp"), lax.axis_index("expert")]).astype(jnp.int32)
    pre = saved_pre.reshape(saved_pre.shape[1:])[0]
    sizes = {name: part * width // 16 for name, part in SIXTEENTHS.items()}
    lead = sizes["a"] + sizes["z"]

    whole = lambda i: (0, 0)
    first = _call(
        functools.partial(_pack_kernel, tokens, lead),
        "pack_tokens",
        pltpu.VMEM((tokens + INFO_ROWS, lead), BF16),
        [
            pl.BlockSpec((routes.shape[1], tokens), whole),
            pl.BlockSpec((routes.shape[1], tokens), whole),
            pl.BlockSpec((tokens, lead), whole),
        ],
        VM,
        PACK_MIB,
        grid=(1,),
    )(*(pltpu.with_memory_space_constraint(v, pltpu.HBM) for v in (routes.T, combine.T, grad_tokens)))
    rest = grad_tokens[:, lead:]

    def gather(block, *later):
        held = {0: block}
        for bit in reversed(range(n_e.bit_length() - 1)):
            for key in sorted(held):
                if later and bit == 0:
                    held[key] = _after(held[key], *later)
                held[key | (1 << bit)] = _send(held[key], 0, 1 << bit)
        return [held[j] for j in range(n_e)]

    firsts = gather(first, rest)

    act = _call(
        functools.partial(_activate_kernel, hidden),
        "activation",
        _shape((n_e, capacity, hidden), F32),
        [VM],
        VM,
        6,
    )(pre)

    last = tuple(range(2, n_d.bit_length() - 1))
    by_x, by_z, at_once = ((0,), (1,), last), ((1,), last, (0,)), ((0,), (1,) + last)

    def blocks_of(stages):
        blocks = [0]
        for b in [b for group in stages for b in group]:
            blocks = [q | (v << b) for q in blocks for v in (0, 1)]
        kept = len(blocks) >> len(stages[0])
        return tuple(blocks[:kept]), tuple(blocks[kept:])

    def halves(kept, sent, size):
        return _shape((kept * rows, size), F32), _shape((sent * rows, size), BF16)

    def exchange(send, size, group):
        got = []
        for v in range(1, 1 << len(group)):
            mask = sum((1 << b) for i, b in enumerate(group) if (v >> (len(group) - 1 - i)) & 1)
            got.append(_send(send[(v - 1) * size : v * size], mask, 0))
        return got

    def merge(keep, got):
        for more in got[:-1]:
            keep = keep + more.astype(F32)
        return keep, got[-1]

    def add(keep, got, group):
        keep, got = merge(keep, got)
        size = keep.shape[0] // rows
        kept = size >> len(group)
        return _call(
            _sum_kernel,
            "sum_halves",
            halves(kept, size - kept, keep.shape[1]),
            [VM, VM],
            (VM, VM),
            8,
        )(keep, got)

    blocks_a, blocks_z = blocks_of(by_x), blocks_of(by_z)
    keep_shape, send_shape = halves(*map(len, blocks_a), sizes["a"])
    at_all, send_a = _call(
        functools.partial(_first_kernel, n_e, n_d, blocks_a[1]),
        "first_send",
        (_shape((hidden, depth), BF16), send_shape),
        [SM] + [VM] * (1 + n_e),
        (VM, VM),
        12,
        0,
        [pltpu.VMEM((hidden, depth), BF16)],
    )(where, act, *firsts)
    keep_a, keep_z, send_z = _call(
        functools.partial(_second_kernel, n_e, blocks_a[0], blocks_z, rows),
        "first_keep",
        (keep_shape,) + halves(*map(len, blocks_z), sizes["z"]),
        [VM] * (1 + n_e),
        (VM,) * 3,
        12,
    )(_after(at_all, send_a), *firsts)
    got_a = exchange(send_a, keep_a.shape[0], by_x[0])
    got_z = exchange(send_z, keep_z.shape[0], by_z[0])

    raw_lead = _call(
        functools.partial(_lead_kernel, n_e, capacity),
        "raw_lead",
        _shape((n_e * capacity, hidden), F32),
        [SM] + [VM] * (1 + n_e),
        VM,
        10,
        LEAD_FLOPS,
        [pltpu.VMEM((n_e * capacity, lead), BF16)],
    )(_after(where, send_a), down_weight, *firsts)

    rests = gather(_after(rest, firsts[n_e // 2]), raw_lead)

    def partial(start, size, stages):
        kept, sent = blocks_of(stages)
        return _call(
            functools.partial(_partial_kernel, n_e, kept, sent, rows, slice(start, start + size)),
            "partial_chunk",
            halves(len(kept), len(sent), size),
            [VM] * (1 + n_e),
            (VM, VM),
            8,
            0,
        )(at_all, *rests)

    keep_b, send_b = partial(0, sizes["b"], by_x)
    keep_c, send_c = partial(sizes["b"], sizes["c"], at_once)

    pre_grad, back = _call(
        functools.partial(_slot_kernel, n_e, hidden),
        "slot_gradients",
        (_shape(pre.shape, BF16), _shape((n_e, 1, tokens), F32)),
        [SM] + [VM] * (3 + 2 * n_e),
        (VM, VM),
        14,
        0,
        [pltpu.VMEM((n_e * capacity, width - lead), BF16)],
    )(_after(where, send_b, send_c), pre, down_weight, raw_lead, *firsts, *rests)
    keep_z, send_z = add(_after(keep_z, back), got_z, by_z[1])
    got_z = exchange(send_z, keep_z.shape[0], by_z[1])
    got_b = exchange(_after(send_b, back, send_z, *got_a), keep_b.shape[0], by_x[0])
    keep_a, send_a = add(_after(keep_a, back), got_a, by_x[1])
    got_a = exchange(send_a, keep_a.shape[0], by_x[1])
    returned = lax.all_to_all(
        _after(back, send_a, send_z), "expert", split_axis=0, concat_axis=0, tiled=True
    )

    got_c = exchange(_after(send_c, returned, *got_b), keep_c.shape[0], at_once[0])
    keep_b, send_b = add(keep_b, got_b, by_x[1])
    got_b = exchange(send_b, keep_b.shape[0], by_x[1])
    keep_a, send_a = add(_after(keep_a, send_b), got_a, by_x[2])
    end_a = [keep_a] + exchange(send_a, keep_a.shape[0], by_x[2])
    keep_z, send_z = add(_after(keep_z, send_a, send_b), got_z, by_z[2])
    end_z = [keep_z] + exchange(send_z, keep_z.shape[0], by_z[2])
    keep_b, send_b = add(keep_b, got_b, by_x[2])
    end_b = [keep_b] + exchange(send_b, keep_b.shape[0], by_x[2])

    keep_c, send_c = add(_after(keep_c, send_b, end_a[1], end_z[1]), got_c, at_once[1])
    end_c = [keep_c] + exchange(send_c, keep_c.shape[0], at_once[1])

    def finish(first_lane, laid_out, ends):
        return _call(
            functools.partial(
                _finish_kernel, 1.0 / n_d, first_lane, tuple(len(end) for end in ends)
            ),
            "finish",
            _shape((rows * lanes, 128), F32),
            [VM] * (len(laid_out) + sum(len(end) for end in ends)),
            VM,
            8,
        )(*laid_out, *[part for end in ends for part in end])

    laid_out = finish(0, [], (end_a, end_z))
    down_grad = finish(lead // 128, [laid_out], (end_b, end_c)).reshape(1, rows * width)

    gate_grad = sum(jnp.where(routes.T == k, returned[k], 0.0) for k in range(n_e)).T
    return pre_grad.reshape(saved_pre.shape), down_grad, gate_grad


def _general(grad_tokens, routes, combine, down_weight, saved_pre):
    experts = lax.axis_size("expert")
    tok_rows, route_count = routes.shape
    capacity = saved_pre.shape[3]
    model_width = grad_tokens.shape[1]
    hidden = down_weight.shape[1]
    flat_routes = routes.reshape(-1)
    onehot = (flat_routes[:, None] == jnp.arange(experts, dtype=jnp.int32)[None, :]).astype(jnp.int32)
    before = jnp.cumsum(onehot, axis=0) - onehot
    position = jnp.sum(before * onehot, axis=1)
    slot_id = flat_routes * capacity + position
    slot_grid = jnp.arange(experts * capacity, dtype=jnp.int32)
    chosen = slot_grid[:, None] == slot_id[None, :]
    placing = jnp.any(chosen.reshape(experts * capacity, tok_rows, route_count), axis=2).astype(BF16)
    outgoing = jnp.dot(placing, grad_tokens, preferred_element_type=F32).astype(BF16)
    combine_flat = combine.reshape(-1).astype(F32)
    out_weight = jnp.sum(jnp.where(chosen, combine_flat[None, :], 0.0), axis=1).astype(BF16)
    swap = functools.partial(lax.all_to_all, axis_name="expert", split_axis=0, concat_axis=0, tiled=True)
    slot_rows = swap(outgoing.reshape(experts, capacity, model_width)).reshape(-1, model_width)
    slot_weight = swap(out_weight.reshape(experts, capacity)).reshape(-1).astype(F32)
    raw_grad = lax.dot_general(
        slot_rows, down_weight[0], (((1,), (1,)), ((), ())), preferred_element_type=F32
    )
    pre_acts = saved_pre.reshape(-1, 2 * hidden).astype(F32)
    gate_pre, up_pre = pre_acts[:, :hidden], pre_acts[:, hidden:]
    logistic = jax.nn.sigmoid(gate_pre)
    activated = gate_pre * logistic
    hidden_act = activated * up_pre
    slot_gate = jnp.sum(hidden_act * raw_grad, axis=1)
    hidden_delta = slot_weight[:, None] * raw_grad
    gate_delta = hidden_delta * up_pre * logistic * (1.0 + gate_pre * (1.0 - logistic))
    pre_grad = jnp.concatenate([gate_delta, hidden_delta * activated], axis=1).astype(BF16)
    scaled = (slot_weight[:, None] * hidden_act).astype(BF16)
    whole_term = lax.dot_general(
        scaled, slot_rows, (((0,), (0,)), ((), ())), preferred_element_type=F32
    )
    summed = lax.psum_scatter(whole_term.reshape(-1), "dp", scatter_dimension=0, tiled=True)
    down_grad = (summed / lax.axis_size("dp"))[None]
    returned_flat = swap(slot_gate.reshape(experts, capacity)).reshape(-1)
    gate_flat = jnp.sum(jnp.where(chosen, returned_flat[:, None], 0.0), axis=0)
    return pre_grad.reshape(saved_pre.shape), down_grad, gate_flat.reshape(tok_rows, route_count)


def solution(mesh):
    n_d, n_e = mesh.shape["dp"], mesh.shape["expert"]

    def per_device(grad_tokens, routes, combine, down_weight, saved_pre):
        hidden, width = down_weight.shape[1:]
        whole_tiles = (
            hidden % (16 * n_d) == 0
            and saved_pre.shape[3] % 16 == 0
            and width % 2048 == 0
            and grad_tokens.shape[0] == 128
            and n_d >= 8
            and n_d & (n_d - 1) == 0
            and n_e >= 2
            and n_e & (n_e - 1) == 0
            and routes.shape[1] == 2
        )
        form = _fast if whole_tiles else _general
        return form(grad_tokens, routes, combine, down_weight, saved_pre)

    by_both = P(("dp", "expert"), None)
    by_expert = P("expert", "dp", None, None, None)
    return jax.shard_map(
        per_device,
        mesh=mesh,
        in_specs=(by_both, by_both, by_both, P("expert", None, None), by_expert),
        out_specs=(by_expert, P("expert", "dp"), by_both),
        check_vma=False,
    )
```

```python
import functools

import jax
import jax.numpy as jnp
from jax import lax
from jax.experimental import pallas as pl
from jax.experimental.pallas import tpu as pltpu
from jax.sharding import PartitionSpec as P

F32 = jnp.float32
BF16 = jnp.bfloat16
AXES = ("dp", "expert")
MIB = 1024 * 1024
INFO_ROWS = 16
PACK_MIB = 8
LEAD_FLOPS = 6 * 10**9
SIXTEENTHS = {"a": 5, "z": 4, "b": 4, "c": 3}


def _send(value, dp_mask, expert_mask):
    dps, experts = lax.axis_size("dp"), lax.axis_size("expert")
    pairs = [
        (d * experts + e, (d ^ dp_mask) * experts + (e ^ expert_mask))
        for d in range(dps)
        for e in range(experts)
    ]
    return lax.ppermute(value, AXES, pairs)


def _choice(info, expert, capacity):
    tokens = info.shape[1]
    first, second = info[0:1, :] == expert, info[1:2, :] == expert
    named = jnp.where(first | second, 1.0, 0.0)
    weight = jnp.where(first, info[2:3, :], 0.0) + jnp.where(second, info[3:4, :], 0.0)
    row = lax.broadcasted_iota(jnp.int32, (tokens, tokens), 0)
    col = lax.broadcasted_iota(jnp.int32, (tokens, tokens), 1)
    earlier = jnp.where(row < col, 1.0, 0.0).astype(BF16)
    position = jnp.dot(
        jnp.broadcast_to(named, (8, tokens)).astype(BF16), earlier, preferred_element_type=F32
    )[0:1, :]
    slot = lax.broadcasted_iota(jnp.int32, (capacity, tokens), 0).astype(F32)
    chosen = jnp.where((slot == position) & (named > 0.0), 1.0, 0.0)
    slot_weight = jnp.sum(chosen * weight, axis=1, keepdims=True)
    return chosen, slot_weight


def _pack_kernel(tokens, lead, routes_ref, combine_ref, tok_ref, first_ref):
    first_ref[0:tokens, :] = tok_ref[...]
    first_ref[tokens:, :] = jnp.zeros((INFO_ROWS, lead), BF16)
    info = jnp.concatenate(
        [
            routes_ref[...].astype(F32),
            combine_ref[...].astype(F32),
            jnp.zeros((INFO_ROWS - 4, tokens), F32),
        ],
        axis=0,
    )
    first_ref[tokens:, 0:tokens] = info.astype(BF16)


def _activate_kernel(hidden, pre_ref, out_ref):
    for j in range(pre_ref.shape[0]):
        pre = pre_ref[j].astype(F32)
        gate, up = pre[:, :hidden], pre[:, hidden:]
        out_ref[j] = gate * jax.nn.sigmoid(gate) * up


def _info(ref, tokens):
    return ref[tokens : tokens + INFO_ROWS, 0:tokens].astype(F32)


def _split(prod, keep_blocks, send_blocks, rows, keep_ref, send_ref):
    for p, q in enumerate(keep_blocks):
        keep_ref[p * rows : (p + 1) * rows, :] = prod[q * rows : (q + 1) * rows, :]
    for p, q in enumerate(send_blocks):
        send_ref[p * rows : (p + 1) * rows, :] = prod[q * rows : (q + 1) * rows, :].astype(BF16)


def _some_rows(at_ref, blocks, rows):
    return jnp.concatenate([at_ref[q * rows : (q + 1) * rows, :] for q in blocks], axis=0)


def _first_kernel(n_e, n_d, sent, where_ref, act_ref, *refs):
    firsts, (at_ref, send_ref, held) = refs[:n_e], refs[n_e:]
    d, e = where_ref[0], where_ref[1]
    expert = e.astype(F32)
    capacity, hidden = act_ref.shape[1:]
    tokens = firsts[0].shape[0] - INFO_ROWS
    rows = hidden // n_d
    none = jnp.zeros((capacity, tokens), F32)
    for j in range(0, n_e, 2):
        left, left_weight = _choice(_info(firsts[j], tokens), expert, capacity)
        right, right_weight = _choice(_info(firsts[j + 1], tokens), expert, capacity)
        scaled = jnp.concatenate(
            [left_weight * act_ref[e ^ j], right_weight * act_ref[e ^ (j + 1)]], axis=0
        ).astype(BF16)
        chosen = jnp.concatenate(
            [
                jnp.concatenate([left, none], axis=1),
                jnp.concatenate([none, right], axis=1),
            ],
            axis=0,
        ).astype(BF16)
        held[:, j * tokens : (j + 2) * tokens] = lax.dot_general(
            scaled, chosen, (((0,), (0,)), ((), ())), preferred_element_type=F32
        ).astype(BF16)
    for q in range(n_d):
        start = pl.multiple_of((d ^ q) * rows, 16)
        at_ref[q * rows : (q + 1) * rows, :] = held[pl.ds(start, rows), :]
    tok = jnp.concatenate([r[0:tokens, : send_ref.shape[1]] for r in firsts], axis=0)
    send_ref[...] = jnp.dot(
        _some_rows(at_ref, sent, rows), tok, preferred_element_type=F32
    ).astype(BF16)


def _second_kernel(n_e, kept, blocks_z, rows, at_ref, *refs):
    firsts, (keep_a_ref, keep_z_ref, send_z_ref) = refs[:n_e], refs[n_e:]
    tokens = firsts[0].shape[0] - INFO_ROWS
    size = keep_a_ref.shape[1]
    tok = jnp.concatenate([r[0:tokens, size:] for r in firsts], axis=0)
    prod = jnp.dot(at_ref[...], tok, preferred_element_type=F32)
    _split(prod, *blocks_z, rows, keep_z_ref, send_z_ref)
    tok = jnp.concatenate([r[0:tokens, :size] for r in firsts], axis=0)
    keep_a_ref[...] = jnp.dot(_some_rows(at_ref, kept, rows), tok, preferred_element_type=F32)


def _partial_kernel(n_e, keep_blocks, send_blocks, rows, columns, at_ref, *refs):
    tok = jnp.concatenate([r[:, columns] for r in refs[:n_e]], axis=0)
    prod = jnp.dot(at_ref[...], tok, preferred_element_type=F32)
    _split(prod, keep_blocks, send_blocks, rows, *refs[n_e:])


def _lead_kernel(n_e, capacity, where_ref, w_ref, *refs):
    firsts, raw_ref, rows_ref = refs[:n_e], refs[n_e], refs[n_e + 1]
    expert = where_ref[1].astype(F32)
    lead = firsts[0].shape[1]
    tokens = firsts[0].shape[0] - INFO_ROWS
    for j in range(n_e):
        chosen, _ = _choice(_info(firsts[j], tokens), expert, capacity)
        rows_ref[j * capacity : (j + 1) * capacity, :] = jnp.dot(
            chosen.astype(BF16), firsts[j][0:tokens, :], preferred_element_type=F32
        ).astype(BF16)
    raw_ref[...] = lax.dot_general(
        rows_ref[...], w_ref[0, :, 0:lead], (((1,), (1,)), ((), ())), preferred_element_type=F32
    )


def _slot_kernel(n_e, hidden, where_ref, pre_ref, w_ref, raw_ref, *refs):
    infos, rests, (pre_grad_ref, back_ref, rows_ref) = refs[:n_e], refs[n_e : 2 * n_e], refs[2 * n_e :]
    e = where_ref[1]
    expert = e.astype(F32)
    capacity = pre_ref.shape[1]
    tokens = rests[0].shape[0]
    lead = infos[0].shape[1]
    picks, weights = [], []
    for j in range(n_e):
        chosen, slot_weight = _choice(_info(infos[j], tokens), expert, capacity)
        picks.append(chosen)
        weights.append(slot_weight)
        rows_ref[j * capacity : (j + 1) * capacity, :] = jnp.dot(
            chosen.astype(BF16), rests[j][...], preferred_element_type=F32
        ).astype(BF16)
    tile = 256 if hidden % 256 == 0 else hidden
    gates = [jnp.zeros((capacity, 1), F32) for _ in range(n_e)]
    for h in range(0, hidden, tile):
        raw_all = raw_ref[:, h : h + tile] + lax.dot_general(
            rows_ref[...],
            w_ref[0, h : h + tile, lead:],
            (((1,), (1,)), ((), ())),
            preferred_element_type=F32,
        )
        for j in range(n_e):
            raw = raw_all[j * capacity : (j + 1) * capacity, :]
            a = pre_ref[e ^ j, :, h : h + tile].astype(F32)
            u = pre_ref[e ^ j, :, hidden + h : hidden + h + tile].astype(F32)
            s = jax.nn.sigmoid(a)
            silu = a * s
            gates[j] = gates[j] + jnp.sum(silu * u * raw, axis=1, keepdims=True)
            delta = weights[j] * raw
            pre_grad_ref[e ^ j, :, h : h + tile] = (delta * u * s * (1.0 + a * (1.0 - s))).astype(BF16)
            pre_grad_ref[e ^ j, :, hidden + h : hidden + h + tile] = (delta * silu).astype(BF16)
    for j in range(n_e):
        back_ref[e ^ j] = jnp.sum(picks[j] * gates[j], axis=0, keepdims=True)


def _sum_kernel(keep_ref, got_ref, next_keep_ref, next_send_ref):
    size = next_keep_ref.shape[0]
    next_keep_ref[...] = keep_ref[0:size, :] + got_ref[0:size, :].astype(F32)
    next_send_ref[...] = (keep_ref[size:, :] + got_ref[size:, :].astype(F32)).astype(BF16)


def _finish_kernel(scale, first_lane, counts, *refs):
    parts, out_ref = refs[:-1], refs[-1]
    rows = parts[-1].shape[0]
    lanes = out_ref.shape[0] // rows
    if first_lane:
        out_ref[...] = parts[0][...]
        parts = parts[1:]
    at = first_lane
    for count in counts:
        total = parts[0][...]
        for more in parts[1:count]:
            total = total + more[...].astype(F32)
        parts = parts[count:]
        total = total * scale
        for j in range(0, total.shape[1], 128):
            out_ref[pl.ds(at, rows, stride=lanes), :] = total[:, j : j + 128]
            at += 1
    if not first_lane:
        for at in range(at, lanes):
            out_ref[pl.ds(at, rows, stride=lanes), :] = jnp.zeros((rows, 128), F32)


def _after(value, *others):
    return lax.optimization_barrier((value,) + others)[0]


VM = pl.BlockSpec(memory_space=pltpu.VMEM)
SM = pl.BlockSpec(memory_space=pltpu.SMEM)


def _call(body, name, outs, in_specs, out_specs, mib, flops=0, scratch=(), **more):
    return pl.pallas_call(
        body,
        out_shape=outs,
        in_specs=in_specs,
        out_specs=out_specs,
        scratch_shapes=scratch,
        compiler_params=pltpu.CompilerParams(vmem_limit_bytes=mib * MIB),
        cost_estimate=pl.CostEstimate(flops=flops, bytes_accessed=0, transcendentals=0),
        name=name,
        **more,
    )


def _shape(shape, dtype):
    return jax.ShapeDtypeStruct(shape, dtype)


def _fast(grad_tokens, routes, combine, down_weight, saved_pre):
    n_d, n_e = lax.axis_size("dp"), lax.axis_size("expert")
    tokens, width = grad_tokens.shape
    hidden = down_weight.shape[1]
    capacity = saved_pre.shape[3]
    rows = hidden // n_d
    depth = n_e * tokens
    lanes = width // 128
    where = jnp.stack([lax.axis_index("dp"), lax.axis_index("expert")]).astype(jnp.int32)
    pre = saved_pre.reshape(saved_pre.shape[1:])[0]
    sizes = {name: part * width // 16 for name, part in SIXTEENTHS.items()}
    lead = sizes["a"] + sizes["z"]

    whole = lambda i: (0, 0)
    first = _call(
        functools.partial(_pack_kernel, tokens, lead),
        "pack_tokens",
        pltpu.VMEM((tokens + INFO_ROWS, lead), BF16),
        [
            pl.BlockSpec((routes.shape[1], tokens), whole),
            pl.BlockSpec((routes.shape[1], tokens), whole),
            pl.BlockSpec((tokens, lead), whole),
        ],
        VM,
        PACK_MIB,
        grid=(1,),
    )(*(pltpu.with_memory_space_constraint(v, pltpu.HBM) for v in (routes.T, combine.T, grad_tokens)))
    rest = grad_tokens[:, lead:]

    def gather(block, *later):
        held = {0: block}
        for bit in reversed(range(n_e.bit_length() - 1)):
            for key in sorted(held):
                if later and bit == 0:
                    held[key] = _after(held[key], *later)
                held[key | (1 << bit)] = _send(held[key], 0, 1 << bit)
        return [held[j] for j in range(n_e)]

    firsts = gather(first, rest)

    act = _call(
        functools.partial(_activate_kernel, hidden),
        "activation",
        _shape((n_e, capacity, hidden), F32),
        [VM],
        VM,
        6,
    )(pre)

    last = tuple(range(2, n_d.bit_length() - 1))
    by_x, by_z, at_once = ((0,), (1,), last), ((1,), last, (0,)), ((0,), (1,) + last)

    def blocks_of(stages):
        blocks = [0]
        for b in [b for group in stages for b in group]:
            blocks = [q | (v << b) for q in blocks for v in (0, 1)]
        kept = len(blocks) >> len(stages[0])
        return tuple(blocks[:kept]), tuple(blocks[kept:])

    def halves(kept, sent, size):
        return _shape((kept * rows, size), F32), _shape((sent * rows, size), BF16)

    def exchange(send, size, group):
        got = []
        for v in range(1, 1 << len(group)):
            mask = sum((1 << b) for i, b in enumerate(group) if (v >> (len(group) - 1 - i)) & 1)
            got.append(_send(send[(v - 1) * size : v * size], mask, 0))
        return got

    def merge(keep, got):
        for more in got[:-1]:
            keep = keep + more.astype(F32)
        return keep, got[-1]

    def add(keep, got, group):
        keep, got = merge(keep, got)
        size = keep.shape[0] // rows
        kept = size >> len(group)
        return _call(
            _sum_kernel,
            "sum_halves",
            halves(kept, size - kept, keep.shape[1]),
            [VM, VM],
            (VM, VM),
            8,
        )(keep, got)

    blocks_a, blocks_z = blocks_of(by_x), blocks_of(by_z)
    keep_shape, send_shape = halves(*map(len, blocks_a), sizes["a"])
    at_all, send_a = _call(
        functools.partial(_first_kernel, n_e, n_d, blocks_a[1]),
        "first_send",
        (_shape((hidden, depth), BF16), send_shape),
        [SM] + [VM] * (1 + n_e),
        (VM, VM),
        12,
        0,
        [pltpu.VMEM((hidden, depth), BF16)],
    )(where, act, *firsts)
    keep_a, keep_z, send_z = _call(
        functools.partial(_second_kernel, n_e, blocks_a[0], blocks_z, rows),
        "first_keep",
        (keep_shape,) + halves(*map(len, blocks_z), sizes["z"]),
        [VM] * (1 + n_e),
        (VM,) * 3,
        12,
    )(_after(at_all, send_a), *firsts)
    got_a = exchange(send_a, keep_a.shape[0], by_x[0])
    got_z = exchange(send_z, keep_z.shape[0], by_z[0])

    raw_lead = _call(
        functools.partial(_lead_kernel, n_e, capacity),
        "raw_lead",
        _shape((n_e * capacity, hidden), F32),
        [SM] + [VM] * (1 + n_e),
        VM,
        10,
        LEAD_FLOPS,
        [pltpu.VMEM((n_e * capacity, lead), BF16)],
    )(_after(where, send_a), down_weight, *firsts)

    rests = gather(_after(rest, firsts[n_e // 2]), raw_lead)

    def partial(start, size, stages):
        kept, sent = blocks_of(stages)
        return _call(
            functools.partial(_partial_kernel, n_e, kept, sent, rows, slice(start, start + size)),
            "partial_chunk",
            halves(len(kept), len(sent), size),
            [VM] * (1 + n_e),
            (VM, VM),
            8,
            0,
        )(at_all, *rests)

    keep_b, send_b = partial(0, sizes["b"], by_x)
    keep_c, send_c = partial(sizes["b"], sizes["c"], at_once)

    pre_grad, back = _call(
        functools.partial(_slot_kernel, n_e, hidden),
        "slot_gradients",
        (_shape(pre.shape, BF16), _shape((n_e, 1, tokens), F32)),
        [SM] + [VM] * (3 + 2 * n_e),
        (VM, VM),
        14,
        0,
        [pltpu.VMEM((n_e * capacity, width - lead), BF16)],
    )(_after(where, send_b, send_c), pre, down_weight, raw_lead, *firsts, *rests)
    keep_z, send_z = add(_after(keep_z, back), got_z, by_z[1])
    got_z = exchange(send_z, keep_z.shape[0], by_z[1])
    got_b = exchange(_after(send_b, back, send_z, *got_a), keep_b.shape[0], by_x[0])
    keep_a, send_a = add(_after(keep_a, back), got_a, by_x[1])
    got_a = exchange(send_a, keep_a.shape[0], by_x[1])
    returned = lax.all_to_all(
        back, "expert", split_axis=0, concat_axis=0, tiled=True
    )

    got_c = exchange(_after(send_c, returned, *got_b), keep_c.shape[0], at_once[0])
    keep_b, send_b = add(keep_b, got_b, by_x[1])
    got_b = exchange(send_b, keep_b.shape[0], by_x[1])
    keep_a, send_a = add(_after(keep_a, send_b), got_a, by_x[2])
    end_a = [keep_a] + exchange(send_a, keep_a.shape[0], by_x[2])
    keep_z, send_z = add(_after(keep_z, send_a, send_b), got_z, by_z[2])
    end_z = [keep_z] + exchange(send_z, keep_z.shape[0], by_z[2])
    keep_b, send_b = add(keep_b, got_b, by_x[2])
    end_b = [keep_b] + exchange(send_b, keep_b.shape[0], by_x[2])

    keep_c, send_c = add(_after(keep_c, send_b, end_a[1], end_z[1]), got_c, at_once[1])
    end_c = [keep_c] + exchange(send_c, keep_c.shape[0], at_once[1])

    def finish(first_lane, laid_out, ends):
        return _call(
            functools.partial(
                _finish_kernel, 1.0 / n_d, first_lane, tuple(len(end) for end in ends)
            ),
            "finish",
            _shape((rows * lanes, 128), F32),
            [VM] * (len(laid_out) + sum(len(end) for end in ends)),
            VM,
            8,
        )(*laid_out, *[part for end in ends for part in end])

    laid_out = finish(0, [], (end_a, end_z))
    down_grad = finish(lead // 128, [laid_out], (end_b, end_c)).reshape(1, rows * width)

    gate_grad = sum(jnp.where(routes.T == k, returned[k], 0.0) for k in range(n_e)).T
    return pre_grad.reshape(saved_pre.shape), down_grad, gate_grad


def _general(grad_tokens, routes, combine, down_weight, saved_pre):
    experts = lax.axis_size("expert")
    tok_rows, route_count = routes.shape
    capacity = saved_pre.shape[3]
    model_width = grad_tokens.shape[1]
    hidden = down_weight.shape[1]
    flat_routes = routes.reshape(-1)
    onehot = (flat_routes[:, None] == jnp.arange(experts, dtype=jnp.int32)[None, :]).astype(jnp.int32)
    before = jnp.cumsum(onehot, axis=0) - onehot
    position = jnp.sum(before * onehot, axis=1)
    slot_id = flat_routes * capacity + position
    slot_grid = jnp.arange(experts * capacity, dtype=jnp.int32)
    chosen = slot_grid[:, None] == slot_id[None, :]
    placing = jnp.any(chosen.reshape(experts * capacity, tok_rows, route_count), axis=2).astype(BF16)
    outgoing = jnp.dot(placing, grad_tokens, preferred_element_type=F32).astype(BF16)
    combine_flat = combine.reshape(-1).astype(F32)
    out_weight = jnp.sum(jnp.where(chosen, combine_flat[None, :], 0.0), axis=1).astype(BF16)
    swap = functools.partial(lax.all_to_all, axis_name="expert", split_axis=0, concat_axis=0, tiled=True)
    slot_rows = swap(outgoing.reshape(experts, capacity, model_width)).reshape(-1, model_width)
    slot_weight = swap(out_weight.reshape(experts, capacity)).reshape(-1).astype(F32)
    raw_grad = lax.dot_general(
        slot_rows, down_weight[0], (((1,), (1,)), ((), ())), preferred_element_type=F32
    )
    pre_acts = saved_pre.reshape(-1, 2 * hidden).astype(F32)
    gate_pre, up_pre = pre_acts[:, :hidden], pre_acts[:, hidden:]
    logistic = jax.nn.sigmoid(gate_pre)
    activated = gate_pre * logistic
    hidden_act = activated * up_pre
    slot_gate = jnp.sum(hidden_act * raw_grad, axis=1)
    hidden_delta = slot_weight[:, None] * raw_grad
    gate_delta = hidden_delta * up_pre * logistic * (1.0 + gate_pre * (1.0 - logistic))
    pre_grad = jnp.concatenate([gate_delta, hidden_delta * activated], axis=1).astype(BF16)
    scaled = (slot_weight[:, None] * hidden_act).astype(BF16)
    whole_term = lax.dot_general(
        scaled, slot_rows, (((0,), (0,)), ((), ())), preferred_element_type=F32
    )
    summed = lax.psum_scatter(whole_term.reshape(-1), "dp", scatter_dimension=0, tiled=True)
    down_grad = (summed / lax.axis_size("dp"))[None]
    returned_flat = swap(slot_gate.reshape(experts, capacity)).reshape(-1)
    gate_flat = jnp.sum(jnp.where(chosen, returned_flat[:, None], 0.0), axis=0)
    return pre_grad.reshape(saved_pre.shape), down_grad, gate_flat.reshape(tok_rows, route_count)


def solution(mesh):
    n_d, n_e = mesh.shape["dp"], mesh.shape["expert"]

    def per_device(grad_tokens, routes, combine, down_weight, saved_pre):
        hidden, width = down_weight.shape[1:]
        whole_tiles = (
            hidden % (16 * n_d) == 0
            and saved_pre.shape[3] % 16 == 0
            and width % 2048 == 0
            and grad_tokens.shape[0] == 128
            and n_d >= 8
            and n_d & (n_d - 1) == 0
            and n_e >= 2
            and n_e & (n_e - 1) == 0
            and routes.shape[1] == 2
        )
        form = _fast if whole_tiles else _general
        return form(grad_tokens, routes, combine, down_weight, saved_pre)

    by_both = P(("dp", "expert"), None)
    by_expert = P("expert", "dp", None, None, None)
    return jax.shard_map(
        per_device,
        mesh=mesh,
        in_specs=(by_both, by_both, by_both, P("expert", None, None), by_expert),
        out_specs=(by_expert, P("expert", "dp"), by_both),
        check_vma=False,
    )
```
